32 devices in a mesh: seq: 8 (over y, x, core), vocab: 4 (over z).
Axes of the slice: x: 2, y: 2, z: 4, core: 2. Of those that a mesh axis runs over, the one named last changes fastest.
Arguments:
- policy_hidden: bfloat16 [2048, 2560], P('seq'), may hold values from -45 to 45
- reference_hidden: bfloat16 [2048, 2560], P('seq'), may hold values from -45 to 45
- targets: int32 [2048], P('seq'), may hold values from 0 to 2559
- lengths: int32 [4], replicated, may hold values from 1 to 1024, 2048 in all
- block_source: int32 [16], P('seq'), may hold values from 0 to 15, each once
- rollout_prompt: int32 [4], replicated, may hold values from 0 to 3, each once
- rollout_slot: int32 [4], replicated, may hold values from 0 to 3, each once
- policy_input_gain: float32 [2560], replicated, may hold values from 0.3 to 3
- policy_query_weight: bfloat16 [2560, 2048], P(None, 'vocab'), may hold values from -0.125 to 0.125
- policy_key_weight: bfloat16 [2560, 512], P(None, 'vocab'), may hold values from -0.125 to 0.125
- policy_value_weight: bfloat16 [2560, 512], P(None, 'vocab'), may hold values from -0.125 to 0.125
- policy_query_gain: float32 [128], replicated, may hold values from 0.5 to 9, as said below
- policy_key_gain: float32 [128], replicated, may hold values from 0.5 to 9, as said below
- policy_out_weight: bfloat16 [2048, 2560], P('vocab'), may hold values from -0.5 to 0.5
- policy_final_gain: float32 [2560], replicated, may hold values from 1.5 to 60, as said below
- policy_head: bfloat16 [2560, 2560], P(None, 'vocab'), may hold values from -0.125 to 0.125
- policy_prompt_keys: bfloat16 [4, 64, 512], P(None, 'seq', 'vocab'), may hold values from -6 to 6
- policy_prompt_values: bfloat16 [4, 64, 512], P(None, 'seq', 'vocab'), may hold values from -6 to 6
- reference_input_gain: float32 [2560], replicated, may hold values from 0.3 to 3
- reference_query_weight: bfloat16 [2560, 2048], P(None, 'vocab'), may hold values from -0.125 to 0.125
- reference_key_weight: bfloat16 [2560, 512], P(None, 'vocab'), may hold values from -0.125 to 0.125
- reference_value_weight: bfloat16 [2560, 512], P(None, 'vocab'), may hold values from -0.125 to 0.125
- reference_query_gain: float32 [128], replicated, may hold values from 0.5 to 9, as said below
- reference_key_gain: float32 [128], replicated, may hold values from 0.5 to 9, as said below
- reference_out_weight: bfloat16 [2048, 2560], P('vocab'), may hold values from -0.5 to 0.5
- reference_final_gain: float32 [2560], replicated, may hold values from 1.5 to 60, as said below
- reference_head: bfloat16 [2560, 2560], P(None, 'vocab'), may hold values from -0.125 to 0.125
- reference_prompt_keys: bfloat16 [4, 64, 512], P(None, 'seq', 'vocab'), may hold values from -6 to 6
- reference_prompt_values: bfloat16 [4, 64, 512], P(None, 'seq', 'vocab'), may hold values from -6 to 6
Outputs:
- token_diff: float32 [2048], P('seq')
- rollout_mean: float32 [4], replicated
The draws below stay inside these ranges and needn't reach their ends.
Inputs may be any that keep to these rules, and one draw needn't show every extreme that they name: `policy_query_gain`: positive. `policy_key_gain`: positive. `reference_query_gain`: positive. `reference_key_gain`: positive. `policy_final_gain`: positive. `reference_final_gain`: positive.
All inputs are finite; a program needn't handle non-finite values.
Results may differ from the reference program's by a relative error of at most 0.04.
The reference program's roundings to bfloat16 on the way count: a program that leaves them out, or rounds other values in their place, can miss the bound.
Values may be sent and summed in bfloat16 or wider, within the bound.
A program may use at most 128 MiB of HBM per device.

```python
import math
import jax
import jax.numpy as jnp
import numpy as np
from jax import lax

D = 2560
HEADS = 16
KV_HEADS = 4
HD = 128
TOK_DEV = 256
BLOCK = 128
ROLLOUTS = 4
TOKENS = 2048
LEN = 1024
NBLK = 16
PROMPTS = 4
PREFIX = 64
VOCAB = 2560
N_SEQ = 8


def log_between(key, shape, low, high):
    unit = jax.random.uniform(key, shape, jnp.float32)
    return jnp.exp(jnp.log(low) + unit * (jnp.log(high) - jnp.log(low)))


def rows_normal(key):
    parts = jax.random.split(key, 3)
    base = jnp.clip(jax.random.normal(parts[0], (TOKENS, D), jnp.float32), -5.0, 5.0)
    row_scale = log_between(parts[1], (TOKENS, 1), 0.3, 3.0)
    col_scale = log_between(parts[2], (1, D), 0.3, 3.0)
    return base * row_scale * col_scale


def draw_policy_hidden(key, part):
    return rows_normal(jax.random.fold_in(key, 1)).astype(jnp.bfloat16)


def draw_reference_hidden(key, part):
    return rows_normal(jax.random.fold_in(key, 2)).astype(jnp.bfloat16)


def gain_drawn(key):
    return log_between(key, (HD,), 0.5, 2.0)


def final_drawn(key):
    return log_between(key, (D,), 1.5, 8.0)


def draw_policy_query_gain(key, part):
    return gain_drawn(jax.random.fold_in(key, 11))


def draw_policy_key_gain(key, part):
    return gain_drawn(jax.random.fold_in(key, 12))


def draw_reference_query_gain(key, part):
    return gain_drawn(jax.random.fold_in(key, 13))


def draw_reference_key_gain(key, part):
    return gain_drawn(jax.random.fold_in(key, 14))


def draw_policy_final_gain(key, part):
    return final_drawn(jax.random.fold_in(key, 21))


def draw_reference_final_gain(key, part):
    return final_drawn(jax.random.fold_in(key, 22))


def place_ends(result, key, least, largest):
    extent = result.shape
    spot = [jax.random.randint(jax.random.fold_in(key, axis), (), 0, extent[axis]) for axis in range(len(extent))]
    result = result.at[tuple(spot)].set(least)
    longest = extent.index(max(extent))
    spot[longest] = (spot[longest] + 1) % extent[longest]
    return result.at[tuple(spot)].set(largest)


def block_scale(own_key, extent, pieces, least, largest):
    factor_of = 1.0
    for dim, blocks in pieces:
        draws = jax.random.uniform(jax.random.fold_in(jax.random.fold_in(own_key, 6), dim), (blocks,), jnp.float32, least / len(pieces), largest / len(pieces))
        factor_of = factor_of * jnp.repeat(jnp.exp(draws), extent[dim] // blocks).reshape((-1,) + (1,) * (len(extent) - 1 - dim))
    return factor_of


def rank_table(number_of, lean):
    portions = [(1 << 20) // math.isqrt(grade ** lean) + 1 for grade in range(1, number_of + 1)]
    deviation = 1 + sum(portions) // (1 << 30)
    return np.cumsum(np.array([max(1, weight // deviation) for weight in portions]))


def ranked(rng, dims, amount, lean):
    table = rank_table(amount, lean)
    pick = jax.random.randint(jax.random.fold_in(rng, 1), dims, 0, int(table[amount - 1]))
    standing = jnp.searchsorted(jnp.asarray(table, jnp.int32), pick, side="right")
    return jax.random.permutation(jax.random.fold_in(rng, 2), amount)[standing].astype(jnp.int32)


def profile(number_of, total, most, lean):
    portions = [(1 << 20) // math.isqrt(rank ** lean) + 1 for rank in range(2, number_of + 1)]
    surplus, given = total - most - (number_of - 1), [1] * (number_of - 1)
    while surplus > 0:
        candidates = [i for i in range(number_of - 1) if given[i] < most]
        whole, remaining = sum([portions[i] for i in candidates]), surplus
        for i in candidates:
            extra = min(most - given[i], max(1, remaining * portions[i] // whole), surplus)
            given[i] = given[i] + extra
            surplus = surplus - extra
    return np.array([most] + given)


def uneven_parts(rng, number_of, total, bound, skew):
    if number_of == 2:
        one = jax.random.randint(rng, (), max(1, total - bound), min(bound, total - 1) + 1)
        return jnp.stack([one, total - one])
    tallies = jnp.asarray(profile(number_of, total, bound, skew), jnp.int32)
    couples = (number_of - 1) // 2
    giver, sink = tallies[1:1 + 2 * couples:2], tallies[2:2 + 2 * couples:2]
    slack = jnp.minimum(giver - 1, bound - sink)
    shifted = jax.random.randint(jax.random.fold_in(rng, 1), (couples,), 0, 1 << 20) % (slack + 1)
    tallies = tallies.at[1:1 + 2 * couples:2].set(giver - shifted).at[2:2 + 2 * couples:2].set(sink + shifted)
    return tallies[jax.random.permutation(jax.random.fold_in(rng, 2), number_of)]


def centred(own_key, dims, width, limit, shards=(), kind=jnp.bfloat16):
    factor_of = block_scale(own_key, dims, shards, -0.22, 0.18) if shards else 1.0
    entries = jax.random.normal(own_key, dims, jnp.float32) * width * factor_of
    return jnp.minimum(jnp.maximum(entries, -limit), limit).astype(kind)


def setup_inputs(seed: int = 0) -> dict:
    arg_keys = jax.random.split(jax.random.key(seed), 30)
    policy_hidden = draw_policy_hidden(jax.random.fold_in(arg_keys[29], 71), 0)
    reference_hidden = draw_reference_hidden(jax.random.fold_in(arg_keys[29], 71), 0)
    targets = place_ends(ranked(arg_keys[2], (TOKENS,), VOCAB, 2), jax.random.fold_in(arg_keys[2], 3), 0, VOCAB - 1).astype(jnp.int32)
    lengths = uneven_parts(arg_keys[3], ROLLOUTS, TOKENS, LEN, 2).astype(jnp.int32)
    block_source = jax.random.permutation(arg_keys[4], NBLK).astype(jnp.int32)
    rollout_prompt = jax.random.permutation(arg_keys[5], PROMPTS).astype(jnp.int32)
    rollout_slot = jax.random.permutation(arg_keys[6], ROLLOUTS).astype(jnp.int32)
    policy_input_gain = jnp.clip(jnp.exp(jax.random.uniform(arg_keys[7], (D,), jnp.float32, math.log(0.3), math.log(3.0))), 0.3, 3.0)
    policy_query_weight = centred(arg_keys[8], (D, HEADS * HD), D ** -0.5, 0.125, ((1, 4),))
    policy_key_weight = centred(arg_keys[9], (D, KV_HEADS * HD), D ** -0.5, 0.125, ((1, 4),))
    policy_value_weight = centred(arg_keys[10], (D, KV_HEADS * HD), D ** -0.5, 0.125, ((1, 4),))
    policy_query_gain = draw_policy_query_gain(jax.random.fold_in(arg_keys[29], 71), 0)
    policy_key_gain = draw_policy_key_gain(jax.random.fold_in(arg_keys[29], 71), 0)
    policy_out_weight = centred(arg_keys[13], (HEADS * HD, D), HD ** -0.5, 0.5, ((0, 4),))
    policy_final_gain = draw_policy_final_gain(jax.random.fold_in(arg_keys[29], 71), 0)
    policy_head = centred(arg_keys[15], (D, VOCAB), D ** -0.5, 0.125, ((1, 4),))
    policy_prompt_keys = centred(arg_keys[16], (PROMPTS, PREFIX, KV_HEADS * HD), 1.0, 6.0, ((1, 8), (2, 4)))
    policy_prompt_values = centred(arg_keys[17], (PROMPTS, PREFIX, KV_HEADS * HD), 1.0, 6.0, ((1, 8), (2, 4)))
    reference_input_gain = jnp.clip(jnp.exp(jax.random.uniform(arg_keys[18], (D,), jnp.float32, math.log(0.3), math.log(3.0))), 0.3, 3.0)
    reference_query_weight = centred(arg_keys[19], (D, HEADS * HD), D ** -0.5, 0.125, ((1, 4),))
    reference_key_weight = centred(arg_keys[20], (D, KV_HEADS * HD), D ** -0.5, 0.125, ((1, 4),))
    reference_value_weight = centred(arg_keys[21], (D, KV_HEADS * HD), D ** -0.5, 0.125, ((1, 4),))
    reference_query_gain = draw_reference_query_gain(jax.random.fold_in(arg_keys[29], 71), 0)
    reference_key_gain = draw_reference_key_gain(jax.random.fold_in(arg_keys[29], 71), 0)
    reference_out_weight = centred(arg_keys[24], (HEADS * HD, D), HD ** -0.5, 0.5, ((0, 4),))
    reference_final_gain = draw_reference_final_gain(jax.random.fold_in(arg_keys[29], 71), 0)
    reference_head = centred(arg_keys[26], (D, VOCAB), D ** -0.5, 0.125, ((1, 4),))
    reference_prompt_keys = centred(arg_keys[27], (PROMPTS, PREFIX, KV_HEADS * HD), 1.0, 6.0, ((1, 8), (2, 4)))
    reference_prompt_values = centred(arg_keys[28], (PROMPTS, PREFIX, KV_HEADS * HD), 1.0, 6.0, ((1, 8), (2, 4)))
    return {"policy_hidden": policy_hidden, "reference_hidden": reference_hidden, "targets": targets, "lengths": lengths, "block_source": block_source, "rollout_prompt": rollout_prompt, "rollout_slot": rollout_slot, "policy_input_gain": policy_input_gain, "policy_query_weight": policy_query_weight, "policy_key_weight": policy_key_weight, "policy_value_weight": policy_value_weight, "policy_query_gain": policy_query_gain, "policy_key_gain": policy_key_gain, "policy_out_weight": policy_out_weight, "policy_final_gain": policy_final_gain, "policy_head": policy_head, "policy_prompt_keys": policy_prompt_keys, "policy_prompt_values": policy_prompt_values, "reference_input_gain": reference_input_gain, "reference_query_weight": reference_query_weight, "reference_key_weight": reference_key_weight, "reference_value_weight": reference_value_weight, "reference_query_gain": reference_query_gain, "reference_key_gain": reference_key_gain, "reference_out_weight": reference_out_weight, "reference_final_gain": reference_final_gain, "reference_head": reference_head, "reference_prompt_keys": reference_prompt_keys, "reference_prompt_values": reference_prompt_values}


EPSILON = 1e-06
ROPE_BASE = 1000000.0
NEGATIVE_FILL = -1e+30

def rms_scale(values, gain_row):
    values = values.astype(jnp.float32)
    return values * lax.rsqrt(lax.optimization_barrier(jnp.mean(values * values, axis=-1, keepdims=True)) + EPSILON) * gain_row.astype(jnp.float32)

def rotate(values, positions):
    half_width = values.shape[-1] // 2
    frequency = ROPE_BASE ** (-2.0 * jnp.arange(half_width, dtype=jnp.float32) / values.shape[-1])
    angles = positions.astype(jnp.float32)[:, None] * frequency[None, :]
    cosine = jnp.cos(angles)
    sine_part = jnp.sin(angles)
    cosine = jnp.concatenate([cosine, cosine], axis=-1)[:, None, :]
    sine_part = jnp.concatenate([sine_part, sine_part], axis=-1)[:, None, :]
    turned = jnp.concatenate([-values[..., half_width:], values[..., :half_width]], axis=-1)
    return values * cosine + turned * sine_part

def layout(block_source, lengths):
    slot_ids = jnp.arange(TOKENS, dtype=jnp.int32)
    packed = block_source[slot_ids // BLOCK] * BLOCK + slot_ids % BLOCK
    end_points = jnp.cumsum(lengths).astype(jnp.int32)
    rollout = lax.optimization_barrier(jnp.sum((packed[:, None] >= end_points[None, :]).astype(jnp.int32), axis=1))
    starts = end_points - lengths
    position = packed - starts[rollout]
    return (rollout.astype(jnp.int32), position.astype(jnp.int32))

def score_model(hidden, rollout, position, prompt_of, targets, input_gain, query_weight, key_weight, value_weight, query_gain, key_gain, out_weight, final_gain, head_weight, prompt_keys, prompt_values):
    group_size = HEADS // KV_HEADS
    normed = rms_scale(hidden, input_gain).astype(jnp.bfloat16)
    rope_position = position + PREFIX
    query_rows = jnp.dot(normed, query_weight, preferred_element_type=jnp.float32).reshape(TOKENS, HEADS, HD)
    query_rows = rotate(rms_scale(query_rows, query_gain), rope_position).astype(jnp.bfloat16)
    key_rows = jnp.dot(normed, key_weight, preferred_element_type=jnp.float32).reshape(TOKENS, KV_HEADS, HD)
    key_rows = rotate(rms_scale(key_rows, key_gain), rope_position).astype(jnp.bfloat16)
    value_rows = jnp.dot(normed, value_weight, preferred_element_type=jnp.float32).astype(jnp.bfloat16).reshape(TOKENS, KV_HEADS, HD)
    all_keys = jnp.concatenate([key_rows, prompt_keys.reshape(PROMPTS * PREFIX, KV_HEADS, HD)], axis=0).astype(jnp.float32)
    all_values = jnp.concatenate([value_rows, prompt_values.reshape(PROMPTS * PREFIX, KV_HEADS, HD)], axis=0).astype(jnp.float32)
    prompt_ids = (jnp.arange(PROMPTS * PREFIX, dtype=jnp.int32) // PREFIX).astype(jnp.int32)
    key_tag = jnp.concatenate([rollout, -1 - prompt_ids])
    key_position = jnp.concatenate([position, jnp.full((PROMPTS * PREFIX,), -1, jnp.int32)])
    scale_factor = HD ** (-0.5)

    def one_block(block_items):
        block_query, block_tag, block_position, block_prompt = block_items
        visible = (key_tag[None, :] == block_tag[:, None]) & (key_position[None, :] <= block_position[:, None]) | (key_tag[None, :] == -1 - block_prompt[:, None])
        shaped = block_query.astype(jnp.float32).reshape(-1, KV_HEADS, group_size, HD)
        scores = jnp.einsum('qkgd,skd->kgqs', shaped, all_keys) * scale_factor
        masked = jnp.where(visible[None, None], scores, NEGATIVE_FILL)
        highest = lax.optimization_barrier(jnp.max(masked, axis=-1, keepdims=True))
        weights = jnp.where(visible[None, None], jnp.exp(scores - highest), 0.0)
        weight_sum = lax.optimization_barrier(jnp.sum(weights, axis=-1))
        rounded = lax.optimization_barrier(weights.astype(jnp.bfloat16)).astype(jnp.float32)
        attended = jnp.einsum('kgqs,skd->qkgd', rounded, all_values) / jnp.transpose(weight_sum, (2, 0, 1))[..., None]
        return attended.reshape(-1, HEADS * HD).astype(jnp.bfloat16)
    attended = lax.map(one_block, (query_rows.reshape(N_SEQ, TOK_DEV, HEADS, HD), rollout.reshape(N_SEQ, TOK_DEV), position.reshape(N_SEQ, TOK_DEV), prompt_of.reshape(N_SEQ, TOK_DEV)))
    attended = attended.reshape(TOKENS, HEADS * HD)
    mixed_rows = jnp.dot(attended, out_weight, preferred_element_type=jnp.float32)
    final_rows = rms_scale(hidden.astype(jnp.float32) + mixed_rows, final_gain).astype(jnp.bfloat16)
    logits = jnp.dot(final_rows, head_weight, preferred_element_type=jnp.float32)
    highest = lax.optimization_barrier(jnp.max(logits, axis=-1))
    log_total = highest + jnp.log(lax.optimization_barrier(jnp.sum(jnp.exp(logits - highest[:, None]), axis=-1)))
    target_logit = jnp.take_along_axis(logits, targets[:, None], axis=1)[:, 0]
    return target_logit - log_total

def reference(policy_hidden, reference_hidden, targets, lengths, block_source, rollout_prompt, rollout_slot, policy_input_gain, policy_query_weight, policy_key_weight, policy_value_weight, policy_query_gain, policy_key_gain, policy_out_weight, policy_final_gain, policy_head, policy_prompt_keys, policy_prompt_values, reference_input_gain, reference_query_weight, reference_key_weight, reference_value_weight, reference_query_gain, reference_key_gain, reference_out_weight, reference_final_gain, reference_head, reference_prompt_keys, reference_prompt_values):
    rollout, position = layout(block_source, lengths)
    prompt_of = rollout_prompt[rollout].astype(jnp.int32)
    policy_score = score_model(policy_hidden, rollout, position, prompt_of, targets, policy_input_gain, policy_query_weight, policy_key_weight, policy_value_weight, policy_query_gain, policy_key_gain, policy_out_weight, policy_final_gain, policy_head, policy_prompt_keys, policy_prompt_values)
    reference_score = score_model(reference_hidden, rollout, position, prompt_of, targets, reference_input_gain, reference_query_weight, reference_key_weight, reference_value_weight, reference_query_gain, reference_key_gain, reference_out_weight, reference_final_gain, reference_head, reference_prompt_keys, reference_prompt_values)
    token_diff = policy_score - reference_score
    per_token = token_diff / lengths[rollout].astype(jnp.float32)
    rollout_sums = jax.ops.segment_sum(per_token, rollout, num_segments=ROLLOUTS)
    rollout_mean = jnp.zeros((ROLLOUTS,), jnp.float32).at[rollout_slot].set(rollout_sums)
    return (token_diff, rollout_mean)
```

```python
import functools

import jax
import jax.numpy as jnp
from jax import lax
from jax.experimental import pallas as pl
from jax.experimental.pallas import tpu as pltpu
from jax.sharding import PartitionSpec as P

HD = 128
BLOCK = 128
EPSILON = 1e-06
ROPE_BASE = 1000000.0
NEGATIVE_FILL = -1e30
CHUNK = 64
MESH = pl.DeviceIdType.MESH
F32 = jnp.float32
BF16 = jnp.bfloat16


def dot(a, b):
    return jnp.dot(a, b, preferred_element_type=F32)


def dot_t(a, b):
    return lax.dot_general(a, b, (((1,), (1,)), ((), ())), preferred_element_type=F32)


def kernel(
    n_seq,
    rolls,
    col_ref,
    row_ref,
    cos_ref,
    sin_ref,
    prompt_ref,
    hid_p,
    hid_r,
    ing_p,
    ing_r,
    qg_p,
    qg_r,
    kg_p,
    kg_r,
    fg_p,
    fg_r,
    wq_p,
    wq_r,
    wk_p,
    wk_r,
    wv_p,
    wv_r,
    wo_p,
    wo_r,
    hd_p,
    hd_r,
    diff_ref,
    mean_ref,
    wq,
    wk,
    wv,
    wo,
    hd,
    hid,
    fgain,
    normed,
    query,
    kv,
    pbuf,
    codes,
    bias,
    mx_s,
    sum_s,
    acc,
    attended,
    part,
    inbuf,
    xs,
    xr,
    own,
    fin,
    stat,
    sbuf,
    rbuf,
    w_sem,
    kv_s,
    kv_r,
    p_s,
    p_r,
    c_s,
    c_r,
    in_s,
    in_r,
    x_s,
    x_r,
    f_s,
    f_r,
    e_s,
    e_r,
    st_s,
    st_r,
    ro_s,
    ro_r,
):
    seq = lax.axis_index("seq")
    voc = lax.axis_index("vocab")
    rows = hid.shape[1]
    width = hid.shape[2]
    heads = query.shape[1]
    n_chips = n_seq // 2
    n_voc = 4
    chip = seq // 2
    core = seq % 2
    sibling = chip * 2 + (1 - core)
    chunks = rows // CHUNK
    total = 2 * chunks
    half = CHUNK // 2
    words = hd.shape[2]
    scale = HD ** (-0.5)

    def remote(src, dst, send, recv, s, v):
        return pltpu.make_async_remote_copy(
            src_ref=src, dst_ref=dst, send_sem=send, recv_sem=recv, device_id=(s, v), device_id_type=MESH
        )

    loads = []
    order = (
        (hid_p, hid, 0), (wk_p, wk, 0), (wv_p, wv, 0), (wq_p, wq, 0),
        (hid_r, hid, 1), (wk_r, wk, 1), (wv_r, wv, 1), (wq_r, wq, 1),
        (wo_p, wo, 0), (wo_r, wo, 1), (hd_p, hd, 0), (hd_r, hd, 1),
    )
    for i, (src, dst, m) in enumerate(order):
        copy = pltpu.make_async_copy(src, dst.at[m], w_sem.at[i])
        copy.start()
        loads.append(copy)

    barrier = pltpu.get_barrier_semaphore()

    def greet_seq(j, carry):
        pl.semaphore_signal(barrier, inc=1, device_id=((seq + j) % n_seq, voc), device_id_type=MESH)
        return carry

    def greet_voc(j, carry):
        pl.semaphore_signal(barrier, inc=1, device_id=(seq, (voc + j) % n_voc), device_id_type=MESH)
        return carry

    lax.fori_loop(1, n_seq, greet_seq, 0)
    lax.fori_loop(1, n_voc, greet_voc, 0)
    fgain[0] = fg_p[...]
    fgain[1] = fg_r[...]
    stat[...] = jnp.zeros_like(stat)
    pbuf[seq] = prompt_ref[...]
    codes[seq] = row_ref[...]
    pl.semaphore_wait(barrier, n_seq - 1 + n_voc - 1)

    def prompt_copy(j):
        peer = (seq + j) % n_seq
        return remote(prompt_ref, pbuf.at[seq], p_s.at[j], p_r.at[seq], peer, voc)

    def code_copy(j):
        peer = (seq + j) % n_seq
        return remote(row_ref, codes.at[seq], c_s.at[j], c_r.at[seq], peer, voc)

    def send_small(j, carry):
        prompt_copy(j).start()
        code_copy(j).start()
        return carry

    lax.fori_loop(1, n_seq, send_small, 0)

    def kv_copy(m, src, dst_seq, slot):
        return remote(kv.at[m, src], kv.at[m, src], kv_s.at[m, slot], kv_r.at[m, src], dst_seq, voc)

    def turn(values, gain):
        values = values * lax.rsqrt(jnp.mean(values * values, axis=-1, keepdims=True) + EPSILON) * gain
        return (values * cos_ref[...] + pltpu.roll(values, HD // 2, axis=1) * sin_ref[...]).astype(BF16)

    for m in range(2):
        ing, qg, kg = ((ing_p, qg_p, kg_p), (ing_r, qg_r, kg_r))[m]
        loads[4 * m].wait()

        def norm_rows(i, carry, m=m, ing=ing):
            here = pl.ds(pl.multiple_of(i * 32, 32), 32)
            values = hid[m, here, :].astype(F32)
            inv = lax.rsqrt(jnp.mean(values * values, axis=-1, keepdims=True) + EPSILON)
            normed[here, :] = (values * inv * ing[...]).astype(BF16)
            return carry

        lax.fori_loop(0, rows // 32, norm_rows, 0)
        loads[4 * m + 1].wait()
        loads[4 * m + 2].wait()
        key_rows = turn(dot(normed[...], wk[m]), kg[...])
        kv[m, seq, :, 0:HD] = key_rows
        kv[m, seq, :, HD : 2 * HD] = dot(normed[...], wv[m]).astype(BF16)
        kv_copy(m, seq, sibling, 0).start()

        def send_kv(j, carry, m=m):
            kv_copy(m, seq, ((chip + j) % n_chips) * 2 + core, j).start()
            return carry

        lax.fori_loop(1, n_chips, send_kv, 0)
        loads[4 * m + 3].wait()
        for h in range(0, heads, 2):
            both = dot(normed[...], wq[m, :, h * HD : (h + 2) * HD])
            query[m, h] = turn(both[:, :HD], qg[...])
            query[m, h + 1] = turn(both[:, HD:], qg[...])

    def wait_small(j, carry):
        src = (seq + n_seq - j) % n_seq
        remote(prompt_ref, pbuf.at[src], p_s.at[j], p_r.at[src], src, voc).wait_recv()
        remote(row_ref, codes.at[src], c_s.at[j], c_r.at[src], src, voc).wait_recv()
        prompt_copy(j).wait_send()
        code_copy(j).wait_send()
        return carry

    lax.fori_loop(1, n_seq, wait_small, 0)
    loads[8].wait()
    loads[9].wait()

    first = col_ref[:, 0:1]
    index = col_ref[:, 1:2]
    prompt = col_ref[:, 2:3]
    prompt_rows = pbuf.shape[2]
    per_prompt = prompt_rows // 4

    def tile(m, src):
        code = codes[src][0:1, :]
        bias[...] = jnp.where((code >= first) & (code <= index), 0.0, NEGATIVE_FILL)

        def head_step(h, carry):
            scores = dot_t(query[m, h], kv[m, src, :, 0:HD]) * scale + bias[...]
            old = mx_s[h]
            new = jnp.maximum(old, jnp.max(scores, axis=-1, keepdims=True))
            weights = jnp.exp(scores - new[:, 0:1])
            factor = jnp.exp(old - new)
            mx_s[h] = new
            sum_s[h] = sum_s[h] * factor + jnp.sum(weights, axis=-1, keepdims=True)
            acc[h] = acc[h] * factor + dot(weights.astype(BF16), kv[m, src, :, HD : 2 * HD])
            return carry

        lax.fori_loop(0, heads, head_step, 0, unroll=True)

    is_end = (voc == 0) | (voc == n_voc - 1)
    middle = 1 + voc // 2
    end = (voc // 2) * 3
    other = 3 - voc

    def rows_of(k, off, count):
        return pl.ds(pl.multiple_of((k % chunks) * CHUNK + off, half), count)

    def partial_chunk(k, store):
        m = k // chunks
        values = attended[m, rows_of(k, 0, CHUNK), :]
        for c in range(0, width, 512):
            store(c, dot(values, wo[m, :, c : c + 512]))

    def in_copy(k):
        m, here = k // chunks, rows_of(k, 0, CHUNK)
        return remote(part.at[m, here, :], inbuf.at[m, here, :], in_s.at[k], in_r.at[k], seq, middle)

    def attend(m, carry):
        prompts = pbuf[:, m].reshape(n_seq * prompt_rows, 2 * HD)
        owner = (lax.broadcasted_iota(jnp.int32, (1, n_seq * prompt_rows), 1) % prompt_rows) // per_prompt
        cover = owner == prompt
        for h in range(heads):
            scores = jnp.where(cover, dot_t(query[m, h], prompts[:, :HD]) * scale, NEGATIVE_FILL)
            top = jnp.max(scores, axis=-1, keepdims=True)
            weights = jnp.exp(scores - top)
            mx_s[h] = jnp.broadcast_to(top, (rows, HD))
            sum_s[h] = jnp.broadcast_to(jnp.sum(weights, axis=-1, keepdims=True), (rows, HD))
            acc[h] = dot(weights.astype(BF16), prompts[:, HD:])

        tile(m, seq)
        kv_copy(m, sibling, sibling, 0).wait_recv()
        tile(m, sibling)

        def chip_step(j, inner):
            src_chip = (chip + n_chips - j) % n_chips
            src = src_chip * 2 + core
            kv_copy(m, src, sibling, 0).wait_recv()
            kv_copy(m, src, sibling, n_chips + j).start()
            tile(m, src)
            src_sib = src_chip * 2 + (1 - core)
            kv_copy(m, src_sib, sibling, 0).wait_recv()
            tile(m, src_sib)
            return inner

        lax.fori_loop(1, n_chips, chip_step, 0)
        for h in range(heads):
            attended[m, :, h * HD : (h + 1) * HD] = (acc[h] / sum_s[h]).astype(BF16)

        @pl.when(is_end)
        def _():
            def send_chunk(i, inner):
                k = m * chunks + i

                def store(c, value):
                    part[m, rows_of(k, 0, CHUNK), c : c + 512] = value.astype(BF16)

                partial_chunk(k, store)
                in_copy(k).start()
                return inner

            lax.fori_loop(0, chunks, send_chunk, 0)

        return carry

    lax.fori_loop(0, 2, attend, 0)
    loads[10].wait()
    loads[11].wait()

    lanes = lax.broadcasted_iota(jnp.int32, (CHUNK, 128), 1)

    def head_chunk(k):
        m, here = k // chunks, rows_of(k, 0, CHUNK)
        logits = dot(fin[m, here, :], hd[m])
        top = jnp.max(logits, axis=-1, keepdims=True)
        mass = jnp.sum(jnp.exp(logits - top), axis=-1, keepdims=True)
        word = voc * words + lax.broadcasted_iota(jnp.int32, (CHUNK, words), 1)
        target = col_ref[here, 3:4]
        hit = jnp.sum(jnp.where(word == target, logits, 0.0), axis=-1, keepdims=True)
        old = stat[here, :]
        old = jnp.where(lanes == 3 * m, top, old)
        old = jnp.where(lanes == 3 * m + 1, mass, old)
        stat[here, :] = jnp.where(lanes == 3 * m + 2, hit, old)

    mine = (voc - 1) * half
    theirs = half - mine

    def x_copy(k):
        return remote(xs.at[k], xr.at[k], x_s.at[k], x_r.at[k], seq, other)

    def f_copy(k, off):
        ref = fin.at[k // chunks, rows_of(k, off, half), :]
        return remote(ref, ref, f_s.at[k], f_r.at[k], seq, other)

    def e_copy(k, off, which):
        ref = fin.at[k // chunks, rows_of(k, off, half), :]
        return remote(ref, ref, e_s.at[2 * k + which], e_r.at[2 * k + which], seq, end)

    @pl.when(is_end)
    def _():
        def step(k, carry):
            first_off = (middle - 1) * half
            for which, off in ((0, first_off), (1, half - first_off)):
                ref = fin.at[k // chunks, rows_of(k, off, half), :]
                remote(ref, ref, e_s.at[2 * k + which], e_r.at[2 * k + which], seq, middle).wait_recv()
            head_chunk(k)
            in_copy(k).wait_send()
            return carry

        lax.fori_loop(0, total, step, 0)

    @pl.when(jnp.logical_not(is_end))
    def _():
        def pass_on(k):
            f_copy(k, theirs).wait_recv()
            e_copy(k, theirs, 1).start()
            head_chunk(k)

        def step(k, carry):
            m = k // chunks

            def store(c, value):
                own[:, c : c + 512] = value

            partial_chunk(k, store)
            pltpu.make_async_remote_copy(
                src_ref=part.at[m, rows_of(k, 0, CHUNK), :],
                dst_ref=inbuf.at[m, rows_of(k, 0, CHUNK), :],
                send_sem=in_s.at[k],
                recv_sem=in_r.at[k],
                device_id=(seq, end),
                device_id_type=MESH,
            ).wait_recv()
            away = pl.ds(pl.multiple_of(theirs, half), half)
            xs[k] = (own[away, :] + inbuf[m, rows_of(k, theirs, half), :].astype(F32)).astype(BF16)
            x_copy(k).start()

            @pl.when(k > 0)
            def _():
                pass_on(k - 1)

            home = pl.ds(pl.multiple_of(mine, half), half)
            here = rows_of(k, mine, half)
            mixed = own[home, :] + inbuf[m, here, :].astype(F32)
            x_copy(k).wait_recv()
            values = hid[m, here, :].astype(F32) + (mixed + xr[k].astype(F32))
            inv = lax.rsqrt(jnp.mean(values * values, axis=-1, keepdims=True) + EPSILON)
            fin[m, here, :] = (values * inv * fgain[m]).astype(BF16)
            f_copy(k, mine).start()
            e_copy(k, mine, 0).start()
            return carry

        lax.fori_loop(0, total, step, 0)
        pass_on(total - 1)

        def drain(k, carry):
            x_copy(k).wait_send()
            f_copy(k, mine).wait_send()
            e_copy(k, mine, 0).wait_send()
            e_copy(k, theirs, 1).wait_send()
            return carry

        lax.fori_loop(0, total, drain, 0)

    sbuf[voc] = jnp.transpose(stat[...])[0:8, :]

    def stat_copy(j):
        return remote(sbuf.at[voc], sbuf.at[voc], st_s.at[j], st_r.at[voc], seq, (voc + j) % n_voc)

    for j in range(1, n_voc):
        stat_copy(j).start()
    for m in range(2):
        def drain_kv(j, carry, m=m):
            kv_copy(m, seq, sibling, j).wait_send()
            return carry

        lax.fori_loop(0, n_chips, drain_kv, 0)
        lax.fori_loop(n_chips + 1, 2 * n_chips, drain_kv, 0)
    for j in range(1, n_voc):
        src = (voc + n_voc - j) % n_voc
        remote(sbuf.at[src], sbuf.at[src], st_s.at[j], st_r.at[src], seq, src).wait_recv()
    parts = [sbuf[v] for v in range(n_voc)]

    def score(m):
        top = functools.reduce(jnp.maximum, [p[3 * m : 3 * m + 1] for p in parts])
        mass = sum(p[3 * m + 1 : 3 * m + 2] * jnp.exp(p[3 * m : 3 * m + 1] - top) for p in parts)
        hit = sum(p[3 * m + 2 : 3 * m + 3] for p in parts)
        return hit - (top + jnp.log(mass))

    diff = score(0) - score(1)
    diff_ref[...] = diff
    per_token = diff / row_ref[2:3, :].astype(F32)
    slot = row_ref[1:2, :]
    lane = lax.broadcasted_iota(jnp.int32, (8, 128), 1)
    block = jnp.zeros((8, 128), F32)
    for r in range(rolls):
        piece = jnp.sum(jnp.where(slot == r, per_token, 0.0), axis=1, keepdims=True)
        block = jnp.where(lane == r, piece, block)
    rbuf[seq] = block

    def roll_copy(j):
        return remote(rbuf.at[seq], rbuf.at[seq], ro_s.at[j], ro_r.at[seq], (seq + j) % n_seq, voc)

    def start_roll(j, carry):
        roll_copy(j).start()
        return carry

    def wait_roll(j, carry):
        src = (seq + n_seq - j) % n_seq
        remote(rbuf.at[src], rbuf.at[src], ro_s.at[j], ro_r.at[src], src, voc).wait_recv()
        return carry

    def drain_roll(j, carry):
        roll_copy(j).wait_send()
        return carry

    lax.fori_loop(1, n_seq, start_roll, 0)
    lax.fori_loop(1, n_seq, wait_roll, 0)
    mean_ref[...] = jnp.sum(rbuf[...], axis=0)
    lax.fori_loop(1, n_seq, drain_roll, 0)
    for j in range(1, n_voc):
        stat_copy(j).wait_send()


def local(
    policy_hidden,
    reference_hidden,
    targets,
    lengths,
    block_source,
    rollout_prompt,
    rollout_slot,
    policy_input_gain,
    policy_query_weight,
    policy_key_weight,
    policy_value_weight,
    policy_query_gain,
    policy_key_gain,
    policy_out_weight,
    policy_final_gain,
    policy_head,
    policy_prompt_keys,
    policy_prompt_values,
    reference_input_gain,
    reference_query_weight,
    reference_key_weight,
    reference_value_weight,
    reference_query_gain,
    reference_key_gain,
    reference_out_weight,
    reference_final_gain,
    reference_head,
    reference_prompt_keys,
    reference_prompt_values,
):
    n_seq = lax.axis_size("seq")
    rows, width = policy_hidden.shape
    rolls = lengths.shape[0]
    heads = policy_query_weight.shape[1] // HD
    words = policy_head.shape[1]
    chunks = rows // CHUNK
    total = 2 * chunks
    prompt_count, prefix_local = policy_prompt_keys.shape[:2]
    prompt_rows = prompt_count * prefix_local

    slot_ids = jnp.arange(rows, dtype=jnp.int32)
    packed = jnp.repeat(block_source, BLOCK) * BLOCK + slot_ids % BLOCK
    ends = jnp.cumsum(lengths)
    rollout = jnp.sum((packed[:, None] >= ends[None, :]).astype(jnp.int32), axis=1)
    member = rollout[:, None] == jnp.arange(rolls, dtype=jnp.int32)[None, :]

    def lookup(table):
        return jnp.sum(jnp.where(member, table[None, :], 0), axis=1)

    first = lookup(ends - lengths)
    zero = jnp.zeros_like(packed)
    col = jnp.stack([first, packed, lookup(rollout_prompt), targets], axis=1)
    col = jnp.pad(col, ((0, 0), (0, 124)))
    row = jnp.stack([packed, lookup(rollout_slot), lookup(lengths), zero, zero, zero, zero, zero], axis=0)
    frequency = ROPE_BASE ** (-2.0 * jnp.arange(HD // 2, dtype=F32) / HD)
    place = packed - first + prefix_local * n_seq
    angles = place.astype(F32)[:, None] * frequency[None, :]
    cosine, sine = jnp.cos(angles), jnp.sin(angles)
    cosine = jnp.concatenate([cosine, cosine], axis=1)
    sine = jnp.concatenate([-sine, sine], axis=1)

    def both(keys, values):
        return jnp.concatenate([keys.reshape(prompt_rows, HD), values.reshape(prompt_rows, HD)], axis=1)

    prompts = jnp.stack(
        [both(policy_prompt_keys, policy_prompt_values), both(reference_prompt_keys, reference_prompt_values)]
    )
    vmem = pl.BlockSpec(memory_space=pltpu.VMEM)
    hbm = pl.BlockSpec(memory_space=pl.ANY)
    dma = pltpu.SemaphoreType.DMA
    n_chips = n_seq // 2
    diff, mean = pl.pallas_call(
        functools.partial(kernel, n_seq, rolls),
        out_shape=(
            jax.ShapeDtypeStruct((1, rows), F32),
            jax.ShapeDtypeStruct((8, 128), F32),
        ),
        in_specs=[vmem] * 5 + [hbm] * 2 + [vmem] * 8 + [hbm] * 10,
        out_specs=(vmem, vmem),
        scratch_shapes=[
            pltpu.VMEM((2, width, heads * HD), BF16),
            pltpu.VMEM((2, width, HD), BF16),
            pltpu.VMEM((2, width, HD), BF16),
            pltpu.VMEM((2, heads * HD, width), BF16),
            pltpu.VMEM((2, width, words), BF16),
            pltpu.VMEM((2, rows, width), BF16),
            pltpu.VMEM((2, 1, width), F32),
            pltpu.VMEM((rows, width), BF16),
            pltpu.VMEM((2, heads, rows, HD), BF16),
            pltpu.VMEM((2, n_seq, rows, 2 * HD), BF16),
            pltpu.VMEM((n_seq, 2, prompt_rows, 2 * HD), BF16),
            pltpu.VMEM((n_seq, 8, rows), jnp.int32),
            pltpu.VMEM((rows, rows), F32),
            pltpu.VMEM((heads, rows, HD), F32),
            pltpu.VMEM((heads, rows, HD), F32),
            pltpu.VMEM((heads, rows, HD), F32),
            pltpu.VMEM((2, rows, heads * HD), BF16),
            pltpu.VMEM((2, rows, width), BF16),
            pltpu.VMEM((2, rows, width), BF16),
            pltpu.VMEM((total, CHUNK // 2, width), BF16),
            pltpu.VMEM((total, CHUNK // 2, width), BF16),
            pltpu.VMEM((CHUNK, width), F32),
            pltpu.VMEM((2, rows, width), BF16),
            pltpu.VMEM((rows, 128), F32),
            pltpu.VMEM((4, 8, rows), F32),
            pltpu.VMEM((n_seq, 8, 128), F32),
            dma((12,)),
            dma((2, n_seq)),
            dma((2, n_seq)),
            dma((n_seq,)),
            dma((n_seq,)),
            dma((n_seq,)),
            dma((n_seq,)),
            dma((total,)),
            dma((total,)),
            dma((total,)),
            dma((total,)),
            dma((total,)),
            dma((total,)),
            dma((2 * total,)),
            dma((2 * total,)),
            dma((4,)),
            dma((4,)),
            dma((n_seq,)),
            dma((n_seq,)),
        ],
        compiler_params=pltpu.CompilerParams(
            collective_id=0, has_side_effects=True, vmem_limit_bytes=60 * 1024 * 1024
        ),
    )(
        col,
        row,
        cosine,
        sine,
        prompts,
        policy_hidden,
        reference_hidden,
        policy_input_gain[None],
        reference_input_gain[None],
        policy_query_gain[None],
        reference_query_gain[None],
        policy_key_gain[None],
        reference_key_gain[None],
        policy_final_gain[None],
        reference_final_gain[None],
        policy_query_weight,
        reference_query_weight,
        policy_key_weight,
        reference_key_weight,
        policy_value_weight,
        reference_value_weight,
        policy_out_weight,
        reference_out_weight,
        policy_head,
        reference_head,
    )
    return (diff.reshape(rows), mean[0, :rolls])


def solution(mesh):
    model_specs = (
        P(),
        P(None, "vocab"),
        P(None, "vocab"),
        P(None, "vocab"),
        P(),
        P(),
        P("vocab", None),
        P(),
        P(None, "vocab"),
        P(None, "seq", "vocab"),
        P(None, "seq", "vocab"),
    )
    return jax.shard_map(
        local,
        mesh=mesh,
        in_specs=(P("seq", None), P("seq", None), P("seq"), P(), P("seq"), P(), P()) + model_specs * 2,
        out_specs=(P("seq"), P()),
        check_vma=False,
    )
```

```python
import functools

import jax
import jax.numpy as jnp
import numpy as np
from jax import lax
from jax.experimental import pallas as pl
from jax.experimental.pallas import tpu as pltpu
from jax.sharding import PartitionSpec as P

HD = 128
BLOCK = 128
EPSILON = 1e-06
ROPE_BASE = 1000000.0
NEGATIVE_FILL = -1e30
CHUNK = 64
MESH = pl.DeviceIdType.MESH
F32 = jnp.float32
BF16 = jnp.bfloat16


def dot(a, b):
    return jnp.dot(a, b, preferred_element_type=F32)


def dot_t(a, b):
    return lax.dot_general(a, b, (((1,), (1,)), ((), ())), preferred_element_type=F32)


def kernel(
    n_seq,
    rolls,
    lens,
    source,
    prompt_of,
    slot_of,
    tgt_ref,
    freq_ref,
    pk_p,
    pv_p,
    pk_r,
    pv_r,
    hid_p,
    hid_r,
    ing_p,
    ing_r,
    qg_p,
    qg_r,
    kg_p,
    kg_r,
    fg_p,
    fg_r,
    wq_p,
    wq_r,
    wk_p,
    wk_r,
    wv_p,
    wv_r,
    wo_p,
    wo_r,
    hd_p,
    hd_r,
    diff_ref,
    mean_ref,
    wq,
    wk,
    wv,
    wo,
    hd,
    hid,
    fgain,
    query,
    kv,
    pbuf,
    codes,
    bias,
    kept,
    col_ref,
    cos_ref,
    sin_ref,
    igain,
    attended,
    inbuf,
    xs,
    xr,
    own,
    keep,
    fin,
    stat,
    sbuf,
    rbuf,
    w_sem,
    kv_s,
    kv_r,
    p_s,
    p_r,
    c_s,
    c_r,
    in_s,
    in_r,
    x_s,
    x_r,
    f_s,
    f_r,
    e_s,
    e_r,
    st_s,
    st_r,
    ro_s,
    ro_r,
):
    seq = lax.axis_index("seq")
    voc = lax.axis_index("vocab")
    rows = hid.shape[1]
    width = hid.shape[2]
    heads = query.shape[1]
    n_chips = n_seq // 2
    n_voc = 4
    chip = seq // 2
    core = seq % 2
    sibling = chip * 2 + (1 - core)
    chunks = rows // CHUNK
    total = 2 * chunks
    half = CHUNK // 2
    words = hd.shape[2]
    scale = HD ** (-0.5)

    def remote(src, dst, send, recv, s, v):
        return pltpu.make_async_remote_copy(
            src_ref=src, dst_ref=dst, send_sem=send, recv_sem=recv, device_id=(s, v), device_id_type=MESH
        )

    loads = []
    order = (
        (hid_p, hid, 0), (wk_p, wk, 0), (wv_p, wv, 0), (wq_p, wq, 0),
        (hid_r, hid, 1), (wk_r, wk, 1), (wv_r, wv, 1), (wq_r, wq, 1),
        (wo_p, wo, 0), (wo_r, wo, 1), (hd_p, hd, 0), (hd_r, hd, 1),
    )
    for i, (src, dst, m) in enumerate(order):
        copy = pltpu.make_async_copy(src, dst.at[m], w_sem.at[i])
        copy.start()
        loads.append(copy)

    barrier = pltpu.get_barrier_semaphore()

    def greet_seq(j, carry):
        pl.semaphore_signal(barrier, inc=1, device_id=((seq + j) % n_seq, voc), device_id_type=MESH)
        return carry

    def greet_voc(j, carry):
        pl.semaphore_signal(barrier, inc=1, device_id=(seq, (voc + j) % n_voc), device_id_type=MESH)
        return carry

    lax.fori_loop(1, n_seq, greet_seq, 0)
    lax.fori_loop(1, n_voc, greet_voc, 0)
    fgain[0] = fg_p[...].reshape(1, width)
    fgain[1] = fg_r[...].reshape(1, width)
    igain[0] = ing_p[...].reshape(1, width)
    igain[1] = ing_r[...].reshape(1, width)
    stat[...] = jnp.zeros_like(stat)
    prompt_rows = pbuf.shape[2]
    per_prompt = pk_p.shape[1]
    for m, (keys, values) in enumerate(((pk_p, pv_p), (pk_r, pv_r))):
        pbuf[seq, m, :, 0:HD] = keys[...].astype(F32).reshape(prompt_rows, HD).astype(BF16)
        pbuf[seq, m, :, HD : 2 * HD] = values[...].astype(F32).reshape(prompt_rows, HD).astype(BF16)

    starts = [jnp.int32(0)]
    for r in range(rolls):
        starts.append(starts[-1] + lens[r])

    def packed_of(slot):
        packed = slot + (source[0] * BLOCK)
        for b in range(1, rows // BLOCK):
            packed = jnp.where(slot >= b * BLOCK, slot + (source[b] - b) * BLOCK, packed)
        return packed

    def lookup(packed, values):
        found = jnp.full_like(packed, 0) + values[0]
        for r in range(1, rolls):
            found = jnp.where(packed >= starts[r], values[r], found)
        return found

    row_code = packed_of(lax.broadcasted_iota(jnp.int32, (8, rows), 1))
    codes[seq] = row_code
    pl.semaphore_wait(barrier, n_seq - 1 + n_voc - 1)

    def prompt_copy(j):
        peer = (seq + j) % n_seq
        return remote(pbuf.at[seq], pbuf.at[seq], p_s.at[j], p_r.at[seq], peer, voc)

    def code_copy(j):
        peer = (seq + j) % n_seq
        return remote(codes.at[seq], codes.at[seq], c_s.at[j], c_r.at[seq], peer, voc)

    def send_small(j, carry):
        prompt_copy(j).start()
        code_copy(j).start()
        return carry

    lax.fori_loop(1, n_seq, send_small, 0)

    packed_col = packed_of(lax.broadcasted_iota(jnp.int32, (rows, 128), 0))
    first_col = lookup(packed_col, starts)
    prompt_col = lookup(packed_col, [prompt_of[r] for r in range(rolls)])
    target_col = jnp.transpose(
        jnp.broadcast_to(tgt_ref[...].reshape(1, rows).astype(F32), (128, rows))
    ).astype(jnp.int32)
    lane_col = lax.broadcasted_iota(jnp.int32, (rows, 128), 1)
    col = jnp.where(lane_col == 0, first_col, packed_col)
    col = jnp.where(lane_col == 2, prompt_col, col)
    col_ref[...] = jnp.where(lane_col == 3, target_col, col)
    place = packed_col - first_col + per_prompt * n_seq
    angles = place.astype(F32) * freq_ref[...]
    cos_ref[...] = jnp.cos(angles)
    sine = jnp.sin(angles)
    sin_ref[...] = jnp.where(lane_col < HD // 2, -sine, sine)

    def kv_copy(m, src, dst_seq, slot):
        return remote(kv.at[m, src], kv.at[m, src], kv_s.at[m, slot], kv_r.at[m, src], dst_seq, voc)

    def turn(values, gain):
        values = values * lax.rsqrt(jnp.mean(values * values, axis=-1, keepdims=True) + EPSILON) * gain
        return (values * cos_ref[...] + pltpu.roll(values, HD // 2, axis=1) * sin_ref[...]).astype(BF16)

    for m in range(2):
        qg, kg = ((qg_p, kg_p), (qg_r, kg_r))[m]
        loads[4 * m].wait()

        def norm_rows(i, carry, m=m):
            here = pl.ds(pl.multiple_of(i * 32, 32), 32)
            values = hid[m, here, :].astype(F32)
            inv = lax.rsqrt(jnp.mean(values * values, axis=-1, keepdims=True) + EPSILON)
            fin[0, here, :] = (values * inv * igain[m]).astype(BF16)
            return carry

        lax.fori_loop(0, rows // 32, norm_rows, 0)
        loads[4 * m + 1].wait()
        loads[4 * m + 2].wait()
        key_rows = turn(dot(fin[0], wk[m]), kg[...])
        kv[m, seq, :, 0:HD] = key_rows
        kv[m, seq, :, HD : 2 * HD] = dot(fin[0], wv[m]).astype(BF16)
        kv_copy(m, seq, sibling, 0).start()

        def send_kv(j, carry, m=m):
            kv_copy(m, seq, ((chip + j) % n_chips) * 2 + core, j).start()
            return carry

        lax.fori_loop(1, n_chips, send_kv, 0)
        loads[4 * m + 3].wait()
        for h in range(0, heads, 2):
            both = dot(fin[0], wq[m, :, h * HD : (h + 2) * HD])
            query[m, h] = turn(both[:, :HD], qg[...])
            query[m, h + 1] = turn(both[:, HD:], qg[...])

    def wait_small(j, carry):
        src = (seq + n_seq - j) % n_seq
        remote(pbuf.at[src], pbuf.at[src], p_s.at[j], p_r.at[src], src, voc).wait_recv()
        remote(codes.at[src], codes.at[src], c_s.at[j], c_r.at[src], src, voc).wait_recv()
        prompt_copy(j).wait_send()
        code_copy(j).wait_send()
        return carry

    lax.fori_loop(1, n_seq, wait_small, 0)
    loads[8].wait()
    loads[9].wait()

    first = col_ref[:, 0:1]
    index = col_ref[:, 1:2]
    prompt = col_ref[:, 2:3]
    prompt_all = n_seq * prompt_rows
    tiles = prompt_all // rows
    per_tile = rows // prompt_rows

    def see(t, carry):
        code = codes[t][0:1, :]
        bias[t] = jnp.where((code >= first) & (code <= index), 0.0, NEGATIVE_FILL)
        return carry

    lax.fori_loop(0, n_seq, see, 0)
    owner = (lax.broadcasted_iota(jnp.int32, (1, rows), 1) % prompt_rows) // per_prompt
    bias[n_seq] = jnp.where(owner == prompt, 0.0, NEGATIVE_FILL)

    def forward_kv(m):
        def chip_step(j, inner):
            src = ((chip + n_chips - j) % n_chips) * 2 + core
            kv_copy(m, src, sibling, 0).wait_recv()
            kv_copy(m, src, sibling, n_chips + j).start()
            return inner

        lax.fori_loop(1, n_chips, chip_step, 0)

    def gathered_kv(m):
        def chip_step(j, inner):
            kv_copy(m, ((chip + n_chips - j) % n_chips) * 2 + (1 - core), sibling, 0).wait_recv()
            return inner

        lax.fori_loop(0, n_chips, chip_step, 0)

    is_end = (voc == 0) | (voc == n_voc - 1)
    middle = 1 + voc // 2
    end = (voc // 2) * 3
    other = 3 - voc

    def rows_of(k, off, count):
        return pl.ds(pl.multiple_of((k % chunks) * CHUNK + off, half), count)

    def partial_chunk(k, store):
        m = k // chunks
        values = attended[m, rows_of(k, 0, CHUNK), :]
        for c in range(0, width, 512):
            store(c, dot(values, wo[m, :, c : c + 512]))

    def in_copy(k):
        m, here = k // chunks, rows_of(k, 0, CHUNK)
        return remote(inbuf.at[m, here, :], inbuf.at[m, here, :], in_s.at[k], in_r.at[k], seq, middle)

    def prompt_tile(m, t):
        here = pl.ds(t * per_tile, per_tile)
        return pbuf[here, m].reshape(rows, 2 * HD)

    def head_step(m, h):
        rate = HD ** (-0.5)
        q = query[m, h]

        def seen(t, high):
            scores = dot_t(q, kv[m, t, :, 0:HD]) + bias[t]
            kept[t] = scores
            return jnp.maximum(high, jnp.maximum(scores[:, :HD], scores[:, HD:]))

        def seen_prompt(t, high):
            scores = dot_t(q, prompt_tile(m, t)[:, 0:HD]) + bias[n_seq]
            kept[n_seq + t] = scores
            return jnp.maximum(high, jnp.maximum(scores[:, :HD], scores[:, HD:]))

        high = jnp.full((rows, HD), NEGATIVE_FILL, F32)
        high = lax.fori_loop(0, tiles, seen_prompt, high)
        high = lax.fori_loop(0, n_seq, seen, high, unroll=2)
        top = jnp.max(high, axis=-1, keepdims=True)

        def weigh(t, values, state):
            mass, total_value = state
            weights = jnp.exp((kept[t] - top) * rate)
            mass = mass + (weights[:, :HD] + weights[:, HD:])
            return (mass, total_value + dot(weights.astype(BF16), values))

        state = (jnp.zeros((rows, HD), F32), jnp.zeros((rows, HD), F32))
        state = lax.fori_loop(
            0, tiles, lambda t, c: weigh(n_seq + t, prompt_tile(m, t)[:, HD:], c), state
        )
        mass, value = lax.fori_loop(
            0, n_seq, lambda t, c: weigh(t, kv[m, t, :, HD : 2 * HD], c), state, unroll=2
        )
        attended[m, :, h * HD : (h + 1) * HD] = (value / jnp.sum(mass, axis=-1, keepdims=True)).astype(BF16)

    forward_kv(0)
    gathered_kv(0)
    for m in range(2):
        if m == 1:
            gathered_kv(1)
        for h in range(heads):
            head_step(m, h)
            if m == 0 and h == heads // 2:
                forward_kv(1)

        @pl.when(is_end)
        def _():
            def send_chunk(i, inner, m=m):
                k = m * chunks + i

                def store(c, value):
                    inbuf[m, rows_of(k, 0, CHUNK), c : c + 512] = value.astype(BF16)

                partial_chunk(k, store)
                in_copy(k).start()
                return inner

            lax.fori_loop(0, chunks, send_chunk, 0)

    loads[10].wait()
    loads[11].wait()

    lanes = lax.broadcasted_iota(jnp.int32, (CHUNK, 128), 1)

    def head_chunk(k):
        m, here = k // chunks, rows_of(k, 0, CHUNK)
        logits = dot(fin[m, here, :], hd[m])
        top = jnp.max(logits, axis=-1, keepdims=True)
        mass = jnp.sum(jnp.exp(logits - top), axis=-1, keepdims=True)
        word = voc * words + lax.broadcasted_iota(jnp.int32, (CHUNK, words), 1)
        target = col_ref[here, 3:4]
        hit = jnp.sum(jnp.where(word == target, logits, 0.0), axis=-1, keepdims=True)
        old = stat[here, :]
        old = jnp.where(lanes == 3 * m, top, old)
        old = jnp.where(lanes == 3 * m + 1, mass, old)
        stat[here, :] = jnp.where(lanes == 3 * m + 2, hit, old)

    mine = (voc - 1) * half
    theirs = half - mine

    def x_copy(k):
        return remote(xs.at[k], xr.at[k], x_s.at[k], x_r.at[k], seq, other)

    def f_copy(k, off):
        ref = fin.at[k // chunks, rows_of(k, off, half), :]
        return remote(ref, ref, f_s.at[k], f_r.at[k], seq, other)

    def e_copy(k, off, which):
        ref = fin.at[k // chunks, rows_of(k, off, half), :]
        return remote(ref, ref, e_s.at[2 * k + which], e_r.at[2 * k + which], seq, end)

    @pl.when(is_end)
    def _():
        def step(k, carry):
            first_off = (middle - 1) * half
            for which, off in ((0, first_off), (1, half - first_off)):
                ref = fin.at[k // chunks, rows_of(k, off, half), :]
                remote(ref, ref, e_s.at[2 * k + which], e_r.at[2 * k + which], seq, middle).wait_recv()
            head_chunk(k)
            in_copy(k).wait_send()
            return carry

        lax.fori_loop(0, total, step, 0)

    @pl.when(jnp.logical_not(is_end))
    def _():
        def pass_on(k):
            f_copy(k, theirs).wait_recv()
            e_copy(k, theirs, 1).start()
            head_chunk(k)

        def step(k, carry):
            m = k // chunks

            def store(c, value):
                own[:, c : c + 512] = value

            partial_chunk(k, store)
            pltpu.make_async_remote_copy(
                src_ref=inbuf.at[m, rows_of(k, 0, CHUNK), :],
                dst_ref=inbuf.at[m, rows_of(k, 0, CHUNK), :],
                send_sem=in_s.at[k],
                recv_sem=in_r.at[k],
                device_id=(seq, end),
                device_id_type=MESH,
            ).wait_recv()
            away = pl.ds(pl.multiple_of(theirs, half), half)
            xs[k] = (own[away, :] + inbuf[m, rows_of(k, theirs, half), :].astype(F32)).astype(BF16)
            x_copy(k).start()

            home = pl.ds(pl.multiple_of(mine, half), half)
            keep[k % 2] = own[home, :] + inbuf[m, rows_of(k, mine, half), :].astype(F32)

            @pl.when(k > 0)
            def _():
                complete(k - 1)

            @pl.when(k > 1)
            def _():
                pass_on(k - 2)

            return carry

        def complete(k):
            m, here = k // chunks, rows_of(k, mine, half)
            x_copy(k).wait_recv()
            values = hid[m, here, :].astype(F32) + (keep[k % 2] + xr[k].astype(F32))
            inv = lax.rsqrt(jnp.mean(values * values, axis=-1, keepdims=True) + EPSILON)
            fin[m, here, :] = (values * inv * fgain[m]).astype(BF16)
            f_copy(k, mine).start()
            e_copy(k, mine, 0).start()

        lax.fori_loop(0, total, step, 0)
        complete(total - 1)
        pass_on(total - 2)
        pass_on(total - 1)

        def drain(k, carry):
            x_copy(k).wait_send()
            f_copy(k, mine).wait_send()
            e_copy(k, mine, 0).wait_send()
            e_copy(k, theirs, 1).wait_send()
            return carry

        lax.fori_loop(0, total, drain, 0)

    sbuf[voc] = jnp.transpose(stat[...])[0:8, :]

    def stat_copy(j):
        return remote(sbuf.at[voc], sbuf.at[voc], st_s.at[j], st_r.at[voc], seq, (voc + j) % n_voc)

    for j in range(1, n_voc):
        stat_copy(j).start()
    for m in range(2):
        def drain_kv(j, carry, m=m):
            kv_copy(m, seq, sibling, j).wait_send()
            return carry

        lax.fori_loop(0, n_chips, drain_kv, 0)
        lax.fori_loop(n_chips + 1, 2 * n_chips, drain_kv, 0)
    for j in range(1, n_voc):
        src = (voc + n_voc - j) % n_voc
        remote(sbuf.at[src], sbuf.at[src], st_s.at[j], st_r.at[src], seq, src).wait_recv()
    parts = [sbuf[v] for v in range(n_voc)]

    def score(m):
        top = functools.reduce(jnp.maximum, [p[3 * m : 3 * m + 1] for p in parts])
        mass = sum(p[3 * m + 1 : 3 * m + 2] * jnp.exp(p[3 * m : 3 * m + 1] - top) for p in parts)
        hit = sum(p[3 * m + 2 : 3 * m + 3] for p in parts)
        return hit - (top + jnp.log(mass))

    diff = score(0) - score(1)
    diff_ref[...] = diff
    packed_row = packed_of(lax.broadcasted_iota(jnp.int32, (1, rows), 1))
    per_token = diff / lookup(packed_row, [lens[r] for r in range(rolls)]).astype(F32)
    slot = lookup(packed_row, [jnp.int32(r) for r in range(rolls)])
    lane = lax.broadcasted_iota(jnp.int32, (8, 128), 1)
    block = jnp.zeros((8, 128), F32)
    for r in range(rolls):
        piece = jnp.sum(jnp.where(slot == r, per_token, 0.0), axis=1, keepdims=True)
        block = jnp.where(lane == slot_of[r], piece, block)
    rbuf[seq] = block

    def roll_copy(j):
        return remote(rbuf.at[seq], rbuf.at[seq], ro_s.at[j], ro_r.at[seq], (seq + j) % n_seq, voc)

    def start_roll(j, carry):
        roll_copy(j).start()
        return carry

    def wait_roll(j, carry):
        src = (seq + n_seq - j) % n_seq
        remote(rbuf.at[src], rbuf.at[src], ro_s.at[j], ro_r.at[src], src, voc).wait_recv()
        return carry

    def drain_roll(j, carry):
        roll_copy(j).wait_send()
        return carry

    lax.fori_loop(1, n_seq, start_roll, 0)
    lax.fori_loop(1, n_seq, wait_roll, 0)
    mean_ref[...] = jnp.sum(rbuf[...], axis=0)
    lax.fori_loop(1, n_seq, drain_roll, 0)
    for j in range(1, n_voc):
        stat_copy(j).wait_send()


def local(
    policy_hidden,
    reference_hidden,
    targets,
    lengths,
    block_source,
    rollout_prompt,
    rollout_slot,
    policy_input_gain,
    policy_query_weight,
    policy_key_weight,
    policy_value_weight,
    policy_query_gain,
    policy_key_gain,
    policy_out_weight,
    policy_final_gain,
    policy_head,
    policy_prompt_keys,
    policy_prompt_values,
    reference_input_gain,
    reference_query_weight,
    reference_key_weight,
    reference_value_weight,
    reference_query_gain,
    reference_key_gain,
    reference_out_weight,
    reference_final_gain,
    reference_head,
    reference_prompt_keys,
    reference_prompt_values,
):
    n_seq = lax.axis_size("seq")
    rows, width = policy_hidden.shape
    rolls = lengths.shape[0]
    heads = policy_query_weight.shape[1] // HD
    words = policy_head.shape[1]
    chunks = rows // CHUNK
    total = 2 * chunks
    prompt_count, prefix_local = policy_prompt_keys.shape[:2]
    prompt_rows = prompt_count * prefix_local

    frequency = ROPE_BASE ** (-2.0 * np.arange(HD // 2, dtype=np.float32) / HD)
    frequency = np.concatenate([frequency, frequency]).astype(np.float32)[None]
    smem = pl.BlockSpec(memory_space=pltpu.SMEM)
    vmem = pl.BlockSpec(memory_space=pltpu.VMEM)
    hbm = pl.BlockSpec(memory_space=pl.ANY)
    dma = pltpu.SemaphoreType.DMA
    n_chips = n_seq // 2
    diff, mean = pl.pallas_call(
        functools.partial(kernel, n_seq, rolls),
        out_shape=(
            jax.ShapeDtypeStruct((1, rows), F32),
            jax.ShapeDtypeStruct((8, 128), F32),
        ),
        in_specs=[smem] * 4 + [vmem] * 6 + [hbm] * 2 + [vmem] * 8 + [hbm] * 10,
        out_specs=(vmem, vmem),
        scratch_shapes=[
            pltpu.VMEM((2, width, heads * HD), BF16),
            pltpu.VMEM((2, width, HD), BF16),
            pltpu.VMEM((2, width, HD), BF16),
            pltpu.VMEM((2, heads * HD, width), BF16),
            pltpu.VMEM((2, width, words), BF16),
            pltpu.VMEM((2, rows, width), BF16),
            pltpu.VMEM((2, 1, width), F32),
            pltpu.VMEM((2, heads, rows, HD), BF16),
            pltpu.VMEM((2, n_seq, rows, 2 * HD), BF16),
            pltpu.VMEM((n_seq, 2, prompt_rows, 2 * HD), BF16),
            pltpu.VMEM((n_seq, 8, rows), jnp.int32),
            pltpu.VMEM((n_seq + 1, rows, rows), F32),
            pltpu.VMEM((n_seq + n_seq * prompt_rows // rows, rows, rows), F32),
            pltpu.VMEM((rows, 128), jnp.int32),
            pltpu.VMEM((rows, 128), F32),
            pltpu.VMEM((rows, 128), F32),
            pltpu.VMEM((2, 1, width), F32),
            pltpu.VMEM((2, rows, heads * HD), BF16),
            pltpu.VMEM((2, rows, width), BF16),
            pltpu.VMEM((total, CHUNK // 2, width), BF16),
            pltpu.VMEM((total, CHUNK // 2, width), BF16),
            pltpu.VMEM((CHUNK, width), F32),
            pltpu.VMEM((2, CHUNK // 2, width), F32),
            pltpu.VMEM((2, rows, width), BF16),
            pltpu.VMEM((rows, 128), F32),
            pltpu.VMEM((4, 8, rows), F32),
            pltpu.VMEM((n_seq, 8, 128), F32),
            dma((12,)),
            dma((2, n_seq)),
            dma((2, n_seq)),
            dma((n_seq,)),
            dma((n_seq,)),
            dma((n_seq,)),
            dma((n_seq,)),
            dma((total,)),
            dma((total,)),
            dma((total,)),
            dma((total,)),
            dma((total,)),
            dma((total,)),
            dma((2 * total,)),
            dma((2 * total,)),
            dma((4,)),
            dma((4,)),
            dma((n_seq,)),
            dma((n_seq,)),
        ],
        compiler_params=pltpu.CompilerParams(
            collective_id=0, has_side_effects=True, vmem_limit_bytes=60 * 1024 * 1024
        ),
    )(
        lengths,
        block_source,
        rollout_prompt,
        rollout_slot,
        targets,
        frequency,
        policy_prompt_keys,
        policy_prompt_values,
        reference_prompt_keys,
        reference_prompt_values,
        policy_hidden,
        reference_hidden,
        policy_input_gain,
        reference_input_gain,
        policy_query_gain[None],
        reference_query_gain[None],
        policy_key_gain[None],
        reference_key_gain[None],
        policy_final_gain,
        reference_final_gain,
        policy_query_weight,
        reference_query_weight,
        policy_key_weight,
        reference_key_weight,
        policy_value_weight,
        reference_value_weight,
        policy_out_weight,
        reference_out_weight,
        policy_head,
        reference_head,
    )
    return (diff.reshape(rows), mean[0, :rolls])


def solution(mesh):
    model_specs = (
        P(),
        P(None, "vocab"),
        P(None, "vocab"),
        P(None, "vocab"),
        P(),
        P(),
        P("vocab", None),
        P(),
        P(None, "vocab"),
        P(None, "seq", "vocab"),
        P(None, "seq", "vocab"),
    )
    return jax.shard_map(
        local,
        mesh=mesh,
        in_specs=(P("seq", None), P("seq", None), P("seq"), P(), P("seq"), P(), P()) + model_specs * 2,
        out_specs=(P("seq"), P()),
        check_vma=False,
    )
```

```python
import functools

import jax
import jax.numpy as jnp
import numpy as np
from jax import lax
from jax.experimental import pallas as pl
from jax.experimental.pallas import tpu as pltpu
from jax.sharding import PartitionSpec as P

HD = 128
BLOCK = 128
EPSILON = 1e-06
ROPE_BASE = 1000000.0
NEGATIVE_FILL = -1e30
CHUNK = 64
MESH = pl.DeviceIdType.MESH
F32 = jnp.float32
BF16 = jnp.bfloat16


def dot(a, b):
    return jnp.dot(a, b, preferred_element_type=F32)


def dot_t(a, b):
    return lax.dot_general(a, b, (((1,), (1,)), ((), ())), preferred_element_type=F32)


def kernel(
    n_seq,
    rolls,
    lens,
    source,
    prompt_of,
    slot_of,
    tgt_ref,
    freq_ref,
    pk_p,
    pv_p,
    pk_r,
    pv_r,
    hid_p,
    hid_r,
    ing_p,
    ing_r,
    qg_p,
    qg_r,
    kg_p,
    kg_r,
    fg_p,
    fg_r,
    wq_p,
    wq_r,
    wk_p,
    wk_r,
    wv_p,
    wv_r,
    wo_p,
    wo_r,
    hd_p,
    hd_r,
    diff_ref,
    mean_ref,
    wq,
    wk,
    wv,
    wo,
    hd,
    hid,
    fgain,
    query,
    kv,
    pbuf,
    codes,
    bias,
    kept,
    col_ref,
    cos_ref,
    sin_ref,
    igain,
    attended,
    inbuf,
    xr,
    own,
    fin,
    stat,
    sbuf,
    rbuf,
    w_sem,
    kv_s,
    kv_r,
    p_s,
    p_r,
    c_s,
    c_r,
    in_s,
    in_r,
    x_s,
    x_r,
    f_s,
    f_r,
    e_s,
    e_r,
    st_s,
    st_r,
    ro_s,
    ro_r,
):
    seq = lax.axis_index("seq")
    voc = lax.axis_index("vocab")
    rows = hid.shape[1]
    width = hid.shape[2]
    heads = query.shape[1]
    n_chips = n_seq // 2
    n_voc = 4
    chip = seq // 2
    core = seq % 2
    sibling = chip * 2 + (1 - core)
    chunks = rows // CHUNK
    total = 2 * chunks
    half = CHUNK // 2
    words = hd.shape[2]
    scale = HD ** (-0.5)

    def remote(src, dst, send, recv, s, v):
        return pltpu.make_async_remote_copy(
            src_ref=src, dst_ref=dst, send_sem=send, recv_sem=recv, device_id=(s, v), device_id_type=MESH
        )

    loads = []
    order = (
        (hid_p, hid, 0), (wk_p, wk, 0), (wv_p, wv, 0), (wq_p, wq, 0),
        (hid_r, hid, 1), (wk_r, wk, 1), (wv_r, wv, 1), (wq_r, wq, 1),
        (wo_p, wo, 0), (wo_r, wo, 1), (hd_p, hd, 0), (hd_r, hd, 1),
    )
    for i, (src, dst, m) in enumerate(order):
        copy = pltpu.make_async_copy(src, dst.at[m], w_sem.at[i])
        loads.append(copy)
    for copy in loads[:4]:
        copy.start()

    barrier = pltpu.get_barrier_semaphore()

    def greet_seq(j, carry):
        pl.semaphore_signal(barrier, inc=1, device_id=((seq + j) % n_seq, voc), device_id_type=MESH)
        return carry

    def greet_voc(j, carry):
        pl.semaphore_signal(barrier, inc=1, device_id=(seq, (voc + j) % n_voc), device_id_type=MESH)
        return carry

    lax.fori_loop(1, n_seq, greet_seq, 0)
    lax.fori_loop(1, n_voc, greet_voc, 0)
    fgain[0] = fg_p[...].reshape(1, width)
    fgain[1] = fg_r[...].reshape(1, width)
    igain[0] = ing_p[...].reshape(1, width)
    igain[1] = ing_r[...].reshape(1, width)
    stat[...] = jnp.zeros_like(stat)
    prompt_rows = pbuf.shape[2]
    per_prompt = pk_p.shape[1]
    for m, (keys, values) in enumerate(((pk_p, pv_p), (pk_r, pv_r))):
        pbuf[seq, m, :, 0:HD] = keys[...].astype(F32).reshape(prompt_rows, HD).astype(BF16)
        pbuf[seq, m, :, HD : 2 * HD] = values[...].astype(F32).reshape(prompt_rows, HD).astype(BF16)

    starts = [jnp.int32(0)]
    for r in range(rolls):
        starts.append(starts[-1] + lens[r])

    def packed_of(slot):
        packed = slot + (source[0] * BLOCK)
        for b in range(1, rows // BLOCK):
            packed = jnp.where(slot >= b * BLOCK, slot + (source[b] - b) * BLOCK, packed)
        return packed

    def lookup(packed, values):
        found = jnp.full_like(packed, 0) + values[0]
        for r in range(1, rolls):
            found = jnp.where(packed >= starts[r], values[r], found)
        return found

    row_code = packed_of(lax.broadcasted_iota(jnp.int32, (8, rows), 1))
    codes[seq] = row_code
    pl.semaphore_wait(barrier, n_seq - 1 + n_voc - 1)

    def prompt_copy(j):
        peer = (seq + j) % n_seq
        return remote(pbuf.at[seq], pbuf.at[seq], p_s.at[j], p_r.at[seq], peer, voc)

    def code_copy(j):
        peer = (seq + j) % n_seq
        return remote(codes.at[seq], codes.at[seq], c_s.at[j], c_r.at[seq], peer, voc)

    def send_small(j, carry):
        prompt_copy(j).start()
        code_copy(j).start()
        return carry

    lax.fori_loop(1, n_seq, send_small, 0)

    packed_col = packed_of(lax.broadcasted_iota(jnp.int32, (rows, 128), 0))
    first_col = lookup(packed_col, starts)
    prompt_col = lookup(packed_col, [prompt_of[r] for r in range(rolls)])
    target_col = jnp.transpose(
        jnp.broadcast_to(tgt_ref[...].reshape(1, rows).astype(F32), (128, rows))
    ).astype(jnp.int32)
    lane_col = lax.broadcasted_iota(jnp.int32, (rows, 128), 1)
    col = jnp.where(lane_col == 0, first_col, packed_col)
    col = jnp.where(lane_col == 2, prompt_col, col)
    col_ref[...] = jnp.where(lane_col == 3, target_col, col)
    place = packed_col - first_col + per_prompt * n_seq
    angles = place.astype(F32) * freq_ref[...]
    cos_ref[...] = jnp.cos(angles)
    sine = jnp.sin(angles)
    sin_ref[...] = jnp.where(lane_col < HD // 2, -sine, sine)

    def kv_copy(m, src, dst_seq, slot):
        return remote(kv.at[m, src], kv.at[m, src], kv_s.at[m, slot], kv_r.at[m, src], dst_seq, voc)

    def turn(values, gain):
        values = values * lax.rsqrt(jnp.mean(values * values, axis=-1, keepdims=True) + EPSILON) * gain
        return (values * cos_ref[...] + pltpu.roll(values, HD // 2, axis=1) * sin_ref[...]).astype(BF16)

    for m in range(2):
        qg, kg = ((qg_p, kg_p), (qg_r, kg_r))[m]
        loads[4 * m].wait()

        def norm_rows(i, carry, m=m):
            here = pl.ds(pl.multiple_of(i * 32, 32), 32)
            values = hid[m, here, :].astype(F32)
            inv = lax.rsqrt(jnp.mean(values * values, axis=-1, keepdims=True) + EPSILON)
            fin[0, here, :] = (values * inv * igain[m]).astype(BF16)
            return carry

        lax.fori_loop(0, rows // 32, norm_rows, 0)
        for copy in loads[4 * (m + 1) : 4 * (m + 2)]:
            copy.start()
        loads[4 * m + 1].wait()
        loads[4 * m + 2].wait()
        key_rows = turn(dot(fin[0], wk[m]), kg[...])
        kv[m, seq, :, 0:HD] = key_rows
        kv[m, seq, :, HD : 2 * HD] = dot(fin[0], wv[m]).astype(BF16)
        kv_copy(m, seq, sibling, 0).start()

        def send_kv(j, carry, m=m):
            kv_copy(m, seq, ((chip + j) % n_chips) * 2 + core, j).start()
            return carry

        lax.fori_loop(1, n_chips, send_kv, 0)
        loads[4 * m + 3].wait()
        for h in range(0, heads, 2):
            both = dot(fin[0], wq[m, :, h * HD : (h + 2) * HD])
            query[m, h] = turn(both[:, :HD], qg[...])
            query[m, h + 1] = turn(both[:, HD:], qg[...])

    def wait_small(j, carry):
        src = (seq + n_seq - j) % n_seq
        remote(pbuf.at[src], pbuf.at[src], p_s.at[j], p_r.at[src], src, voc).wait_recv()
        remote(codes.at[src], codes.at[src], c_s.at[j], c_r.at[src], src, voc).wait_recv()
        prompt_copy(j).wait_send()
        code_copy(j).wait_send()
        return carry

    lax.fori_loop(1, n_seq, wait_small, 0)
    loads[8].wait()
    loads[9].wait()

    first = col_ref[:, 0:1]
    index = col_ref[:, 1:2]
    prompt = col_ref[:, 2:3]
    prompt_all = n_seq * prompt_rows
    tiles = prompt_all // rows
    per_tile = rows // prompt_rows

    def see(t, carry):
        code = codes[t][0:1, :]
        bias[t] = jnp.where((code >= first) & (code <= index), 0.0, NEGATIVE_FILL)
        return carry

    lax.fori_loop(0, n_seq, see, 0)
    owner = (lax.broadcasted_iota(jnp.int32, (1, rows), 1) % prompt_rows) // per_prompt
    bias[n_seq] = jnp.where(owner == prompt, 0.0, NEGATIVE_FILL)

    def forward_kv(m):
        def chip_step(j, inner):
            src = ((chip + n_chips - j) % n_chips) * 2 + core
            kv_copy(m, src, sibling, 0).wait_recv()
            kv_copy(m, src, sibling, n_chips + j).start()
            return inner

        lax.fori_loop(1, n_chips, chip_step, 0)

    def gathered_kv(m):
        def chip_step(j, inner):
            kv_copy(m, ((chip + n_chips - j) % n_chips) * 2 + (1 - core), sibling, 0).wait_recv()
            return inner

        lax.fori_loop(0, n_chips, chip_step, 0)

    is_end = (voc == 0) | (voc == n_voc - 1)
    middle = 1 + voc // 2
    end = (voc // 2) * 3
    other = 3 - voc

    def rows_of(k, off, count):
        return pl.ds(pl.multiple_of((k % chunks) * CHUNK + off, half), count)

    def partial_sums(m, out):
        values = attended[m]
        for c in range(0, width, 512):
            out[m, :, c : c + 512] = dot(values, wo[m, :, c : c + 512]).astype(BF16)

    def in_copy(k):
        m, here = k // chunks, rows_of(k, 0, CHUNK)
        return remote(inbuf.at[m, here, :], inbuf.at[m, here, :], in_s.at[k], in_r.at[k], seq, middle)

    def prompt_tile(m, t):
        here = pl.ds(t * per_tile, per_tile)
        return pbuf[here, m].reshape(rows, 2 * HD)

    def head_step(m, h):
        rate = HD ** (-0.5)
        q = query[m, h]

        def seen(t, high):
            scores = dot_t(q, kv[m, t, :, 0:HD]) + bias[t]
            kept[t] = scores
            return jnp.maximum(high, jnp.maximum(scores[:, :HD], scores[:, HD:]))

        def seen_prompt(t, high):
            scores = dot_t(q, prompt_tile(m, t)[:, 0:HD]) + bias[n_seq]
            kept[n_seq + t] = scores
            return jnp.maximum(high, jnp.maximum(scores[:, :HD], scores[:, HD:]))

        high = jnp.full((rows, HD), NEGATIVE_FILL, F32)
        high = lax.fori_loop(0, tiles, seen_prompt, high)
        high = lax.fori_loop(0, n_seq, seen, high, unroll=2)
        top = jnp.max(high, axis=-1, keepdims=True)

        def weigh(t, values, state):
            mass, total_value = state
            weights = jnp.exp((kept[t] - top) * rate)
            mass = mass + (weights[:, :HD] + weights[:, HD:])
            return (mass, total_value + dot(weights.astype(BF16), values))

        state = (jnp.zeros((rows, HD), F32), jnp.zeros((rows, HD), F32))
        state = lax.fori_loop(
            0, tiles, lambda t, c: weigh(n_seq + t, prompt_tile(m, t)[:, HD:], c), state
        )
        mass, value = lax.fori_loop(
            0, n_seq, lambda t, c: weigh(t, kv[m, t, :, HD : 2 * HD], c), state, unroll=2
        )
        attended[m, :, h * HD : (h + 1) * HD] = (value / jnp.sum(mass, axis=-1, keepdims=True)).astype(BF16)

    forward_kv(0)
    gathered_kv(0)
    for m in range(2):
        if m == 1:
            gathered_kv(1)
        for h in range(heads):
            head_step(m, h)
            if m == 0 and h == heads // 2:
                forward_kv(1)

        @pl.when(is_end)
        def _(m=m):
            partial_sums(m, inbuf)
            if m == 0:
                in_copy(0).start()
                in_copy(1).start()

        @pl.when(jnp.logical_not(is_end))
        def _(m=m):
            partial_sums(m, own)

    loads[10].wait()
    loads[11].wait()

    lanes = lax.broadcasted_iota(jnp.int32, (2 * CHUNK, 128), 1)

    def head_pair(k):
        m, here = k // chunks, rows_of(k, 0, 2 * CHUNK)
        logits = dot(fin[m, here, :], hd[m])
        top = jnp.max(logits, axis=-1, keepdims=True)
        mass = jnp.sum(jnp.exp(logits - top), axis=-1, keepdims=True)
        word = voc * words + lax.broadcasted_iota(jnp.int32, (2 * CHUNK, words), 1)
        target = col_ref[here, 3:4]
        hit = jnp.sum(jnp.where(word == target, logits, 0.0), axis=-1, keepdims=True)
        old = stat[here, :]
        old = jnp.where(lanes == 3 * m, top, old)
        old = jnp.where(lanes == 3 * m + 1, mass, old)
        stat[here, :] = jnp.where(lanes == 3 * m + 2, hit, old)

    mine = (voc - 1) * half
    theirs = half - mine

    def x_copy(k):
        return remote(inbuf.at[k // chunks, rows_of(k, theirs, half), :], xr.at[k], x_s.at[k], x_r.at[k], seq, other)

    def f_copy(k, off):
        ref = fin.at[k // chunks, rows_of(k, off, half), :]
        return remote(ref, ref, f_s.at[k], f_r.at[k], seq, other)

    def e_copy(k, off, which):
        ref = fin.at[k // chunks, rows_of(k, off, half), :]
        return remote(ref, ref, e_s.at[2 * k + which], e_r.at[2 * k + which], seq, end)

    @pl.when(is_end)
    def _():
        def issue(k, carry):
            in_copy(k - 2).wait_send()
            in_copy(k).start()
            return carry

        lax.fori_loop(2, total, issue, 0)
        first_off = (middle - 1) * half

        def landed(k):
            for which, off in ((0, first_off), (1, half - first_off)):
                ref = fin.at[k // chunks, rows_of(k, off, half), :]
                remote(ref, ref, e_s.at[2 * k + which], e_r.at[2 * k + which], seq, middle).wait_recv()

        def step(i, carry):
            landed(2 * i)
            landed(2 * i + 1)
            head_pair(2 * i)
            return carry

        lax.fori_loop(0, total // 2, step, 0)
        in_copy(total - 2).wait_send()
        in_copy(total - 1).wait_send()

    @pl.when(jnp.logical_not(is_end))
    def _():
        def pass_on(k):
            f_copy(k, theirs).wait_recv()
            e_copy(k, theirs, 1).start()

            @pl.when(k % 2 == 1)
            def _():
                head_pair(k - 1)

        def step(k, carry):
            m = k // chunks
            pltpu.make_async_remote_copy(
                src_ref=inbuf.at[m, rows_of(k, 0, CHUNK), :],
                dst_ref=inbuf.at[m, rows_of(k, 0, CHUNK), :],
                send_sem=in_s.at[k],
                recv_sem=in_r.at[k],
                device_id=(seq, end),
                device_id_type=MESH,
            ).wait_recv()
            away = rows_of(k, theirs, half)
            inbuf[m, away, :] = (own[m, away, :].astype(F32) + inbuf[m, away, :].astype(F32)).astype(BF16)
            x_copy(k).start()

            @pl.when(k > 0)
            def _():
                complete(k - 1)

            @pl.when(k > 1)
            def _():
                pass_on(k - 2)

            return carry

        def complete(k):
            m, here = k // chunks, rows_of(k, mine, half)
            x_copy(k).wait_recv()
            mixed = own[m, here, :].astype(F32) + inbuf[m, here, :].astype(F32)
            values = hid[m, here, :].astype(F32) + (mixed + xr[k].astype(F32))
            inv = lax.rsqrt(jnp.mean(values * values, axis=-1, keepdims=True) + EPSILON)
            fin[m, here, :] = (values * inv * fgain[m]).astype(BF16)
            f_copy(k, mine).start()
            e_copy(k, mine, 0).start()

        lax.fori_loop(0, total, step, 0)
        complete(total - 1)
        pass_on(jnp.int32(total - 2))
        pass_on(jnp.int32(total - 1))

        def drain(k, carry):
            x_copy(k).wait_send()
            f_copy(k, mine).wait_send()
            e_copy(k, mine, 0).wait_send()
            e_copy(k, theirs, 1).wait_send()
            return carry

        lax.fori_loop(0, total, drain, 0)

    sbuf[voc] = jnp.transpose(stat[...])[0:8, :]

    def stat_copy(j):
        return remote(sbuf.at[voc], sbuf.at[voc], st_s.at[j], st_r.at[voc], seq, (voc + j) % n_voc)

    for j in range(1, n_voc):
        stat_copy(j).start()
    for m in range(2):
        def drain_kv(j, carry, m=m):
            kv_copy(m, seq, sibling, j).wait_send()
            return carry

        lax.fori_loop(0, n_chips, drain_kv, 0)
        lax.fori_loop(n_chips + 1, 2 * n_chips, drain_kv, 0)
    for j in range(1, n_voc):
        src = (voc + n_voc - j) % n_voc
        remote(sbuf.at[src], sbuf.at[src], st_s.at[j], st_r.at[src], seq, src).wait_recv()
    parts = [sbuf[v] for v in range(n_voc)]

    def score(m):
        top = functools.reduce(jnp.maximum, [p[3 * m : 3 * m + 1] for p in parts])
        mass = sum(p[3 * m + 1 : 3 * m + 2] * jnp.exp(p[3 * m : 3 * m + 1] - top) for p in parts)
        hit = sum(p[3 * m + 2 : 3 * m + 3] for p in parts)
        return hit - (top + jnp.log(mass))

    diff = score(0) - score(1)
    diff_ref[...] = diff.reshape(rows)
    packed_row = packed_of(lax.broadcasted_iota(jnp.int32, (1, rows), 1))
    per_token = diff / lookup(packed_row, [lens[r] for r in range(rolls)]).astype(F32)
    slot = lookup(packed_row, [jnp.int32(r) for r in range(rolls)])
    lane = lax.broadcasted_iota(jnp.int32, (8, 128), 1)
    block = jnp.zeros((8, 128), F32)
    for r in range(rolls):
        piece = jnp.sum(jnp.where(slot == r, per_token, 0.0), axis=1, keepdims=True)
        block = jnp.where(lane == slot_of[r], piece, block)
    rbuf[seq] = block

    def roll_copy(j):
        return remote(rbuf.at[seq], rbuf.at[seq], ro_s.at[j], ro_r.at[seq], (seq + j) % n_seq, voc)

    def start_roll(j, carry):
        roll_copy(j).start()
        return carry

    def wait_roll(j, carry):
        src = (seq + n_seq - j) % n_seq
        remote(rbuf.at[src], rbuf.at[src], ro_s.at[j], ro_r.at[src], src, voc).wait_recv()
        return carry

    def drain_roll(j, carry):
        roll_copy(j).wait_send()
        return carry

    lax.fori_loop(1, n_seq, start_roll, 0)
    lax.fori_loop(1, n_seq, wait_roll, 0)
    means = jnp.sum(rbuf[...], axis=0)
    for r in range(rolls):
        mean_ref[r] = means[0, r]
    lax.fori_loop(1, n_seq, drain_roll, 0)
    for j in range(1, n_voc):
        stat_copy(j).wait_send()


def local(
    policy_hidden,
    reference_hidden,
    targets,
    lengths,
    block_source,
    rollout_prompt,
    rollout_slot,
    policy_input_gain,
    policy_query_weight,
    policy_key_weight,
    policy_value_weight,
    policy_query_gain,
    policy_key_gain,
    policy_out_weight,
    policy_final_gain,
    policy_head,
    policy_prompt_keys,
    policy_prompt_values,
    reference_input_gain,
    reference_query_weight,
    reference_key_weight,
    reference_value_weight,
    reference_query_gain,
    reference_key_gain,
    reference_out_weight,
    reference_final_gain,
    reference_head,
    reference_prompt_keys,
    reference_prompt_values,
):
    n_seq = lax.axis_size("seq")
    rows, width = policy_hidden.shape
    rolls = lengths.shape[0]
    heads = policy_query_weight.shape[1] // HD
    words = policy_head.shape[1]
    chunks = rows // CHUNK
    total = 2 * chunks
    prompt_count, prefix_local = policy_prompt_keys.shape[:2]
    prompt_rows = prompt_count * prefix_local

    frequency = ROPE_BASE ** (-2.0 * np.arange(HD // 2, dtype=np.float32) / HD)
    frequency = np.concatenate([frequency, frequency]).astype(np.float32)[None]
    smem = pl.BlockSpec(memory_space=pltpu.SMEM)
    vmem = pl.BlockSpec(memory_space=pltpu.VMEM)
    hbm = pl.BlockSpec(memory_space=pl.ANY)
    dma = pltpu.SemaphoreType.DMA
    n_chips = n_seq // 2
    return pl.pallas_call(
        functools.partial(kernel, n_seq, rolls),
        out_shape=(
            jax.ShapeDtypeStruct((rows,), F32),
            jax.ShapeDtypeStruct((rolls,), F32),
        ),
        in_specs=[smem] * 4 + [vmem] * 6 + [hbm] * 2 + [vmem] * 8 + [hbm] * 10,
        out_specs=(vmem, smem),
        scratch_shapes=[
            pltpu.VMEM((2, width, heads * HD), BF16),
            pltpu.VMEM((2, width, HD), BF16),
            pltpu.VMEM((2, width, HD), BF16),
            pltpu.VMEM((2, heads * HD, width), BF16),
            pltpu.VMEM((2, width, words), BF16),
            pltpu.VMEM((2, rows, width), BF16),
            pltpu.VMEM((2, 1, width), F32),
            pltpu.VMEM((2, heads, rows, HD), BF16),
            pltpu.VMEM((2, n_seq, rows, 2 * HD), BF16),
            pltpu.VMEM((n_seq, 2, prompt_rows, 2 * HD), BF16),
            pltpu.VMEM((n_seq, 8, rows), jnp.int32),
            pltpu.VMEM((n_seq + 1, rows, rows), F32),
            pltpu.VMEM((n_seq + n_seq * prompt_rows // rows, rows, rows), F32),
            pltpu.VMEM((rows, 128), jnp.int32),
            pltpu.VMEM((rows, 128), F32),
            pltpu.VMEM((rows, 128), F32),
            pltpu.VMEM((2, 1, width), F32),
            pltpu.VMEM((2, rows, heads * HD), BF16),
            pltpu.VMEM((2, rows, width), BF16),
            pltpu.VMEM((total, CHUNK // 2, width), BF16),
            pltpu.VMEM((2, rows, width), BF16),
            pltpu.VMEM((2, rows, width), BF16),
            pltpu.VMEM((rows, 128), F32),
            pltpu.VMEM((4, 8, rows), F32),
            pltpu.VMEM((n_seq, 8, 128), F32),
            dma((12,)),
            dma((2, n_seq)),
            dma((2, n_seq)),
            dma((n_seq,)),
            dma((n_seq,)),
            dma((n_seq,)),
            dma((n_seq,)),
            dma((total,)),
            dma((total,)),
            dma((total,)),
            dma((total,)),
            dma((total,)),
            dma((total,)),
            dma((2 * total,)),
            dma((2 * total,)),
            dma((4,)),
            dma((4,)),
            dma((n_seq,)),
            dma((n_seq,)),
        ],
        compiler_params=pltpu.CompilerParams(
            collective_id=0, has_side_effects=True, vmem_limit_bytes=60 * 1024 * 1024
        ),
    )(
        lengths,
        block_source,
        rollout_prompt,
        rollout_slot,
        targets,
        frequency,
        policy_prompt_keys,
        policy_prompt_values,
        reference_prompt_keys,
        reference_prompt_values,
        policy_hidden,
        reference_hidden,
        policy_input_gain,
        reference_input_gain,
        policy_query_gain[None],
        reference_query_gain[None],
        policy_key_gain[None],
        reference_key_gain[None],
        policy_final_gain,
        reference_final_gain,
        policy_query_weight,
        reference_query_weight,
        policy_key_weight,
        reference_key_weight,
        policy_value_weight,
        reference_value_weight,
        policy_out_weight,
        reference_out_weight,
        policy_head,
        reference_head,
    )


def solution(mesh):
    model_specs = (
        P(),
        P(None, "vocab"),
        P(None, "vocab"),
        P(None, "vocab"),
        P(),
        P(),
        P("vocab", None),
        P(),
        P(None, "vocab"),
        P(None, "seq", "vocab"),
        P(None, "seq", "vocab"),
    )
    return jax.shard_map(
        local,
        mesh=mesh,
        in_specs=(P("seq", None), P("seq", None), P("seq"), P(), P("seq"), P(), P()) + model_specs * 2,
        out_specs=(P("seq"), P()),
        check_vma=False,
    )
```

```python
import functools

import jax
import jax.numpy as jnp
import numpy as np
from jax import lax
from jax.experimental import pallas as pl
from jax.experimental.pallas import tpu as pltpu
from jax.sharding import PartitionSpec as P

HD = 128
BLOCK = 128
EPSILON = 1e-06
ROPE_BASE = 1000000.0
NEGATIVE_FILL = -1e30
CHUNK = 32
MESH = pl.DeviceIdType.MESH
F32 = jnp.float32
BF16 = jnp.bfloat16


def dot(a, b):
    return jnp.dot(a, b, preferred_element_type=F32)


def dot_t(a, b):
    return lax.dot_general(a, b, (((1,), (1,)), ((), ())), preferred_element_type=F32)


def kernel(
    n_seq,
    rolls,
    lens,
    source,
    prompt_of,
    slot_of,
    tgt_ref,
    freq_ref,
    pk_p,
    pv_p,
    pk_r,
    pv_r,
    hid_p,
    hid_r,
    ing_p,
    ing_r,
    qg_p,
    qg_r,
    kg_p,
    kg_r,
    fg_p,
    fg_r,
    wq_p,
    wq_r,
    wk_p,
    wk_r,
    wv_p,
    wv_r,
    wo_p,
    wo_r,
    hd_p,
    hd_r,
    diff_ref,
    mean_ref,
    wq,
    wk,
    wv,
    wo,
    hd,
    hid,
    fgain,
    query,
    kv,
    pbuf,
    codes,
    bias,
    kept,
    col_ref,
    cos_ref,
    sin_ref,
    igain,
    attended,
    inbuf,
    xr,
    own,
    fin,
    stat,
    sbuf,
    rbuf,
    w_sem,
    kv_s,
    kv_r,
    p_s,
    p_r,
    c_s,
    c_r,
    in_s,
    in_r,
    x_s,
    x_r,
    f_s,
    f_r,
    e_s,
    e_r,
    st_s,
    st_r,
    ro_s,
    ro_r,
):
    seq = lax.axis_index("seq")
    voc = lax.axis_index("vocab")
    rows = hid.shape[1]
    width = hid.shape[2]
    heads = query.shape[1]
    n_chips = n_seq // 2
    n_voc = 4
    chip = seq // 2
    core = seq % 2
    sibling = chip * 2 + (1 - core)
    chunks = rows // CHUNK
    total = 2 * chunks
    half = CHUNK // 2
    words = hd.shape[2]
    scale = HD ** (-0.5)

    def remote(src, dst, send, recv, s, v):
        return pltpu.make_async_remote_copy(
            src_ref=src, dst_ref=dst, send_sem=send, recv_sem=recv, device_id=(s, v), device_id_type=MESH
        )

    loads = []
    order = (
        (hid_p, hid, 0), (wk_p, wk, 0), (wv_p, wv, 0), (wq_p, wq, 0),
        (hid_r, hid, 1), (wk_r, wk, 1), (wv_r, wv, 1), (wq_r, wq, 1),
        (wo_p, wo, 0), (wo_r, wo, 1), (hd_p, hd, 0), (hd_r, hd, 1),
    )
    for i, (src, dst, m) in enumerate(order):
        copy = pltpu.make_async_copy(src, dst.at[m], w_sem.at[i])
        loads.append(copy)
    for copy in loads[:4]:
        copy.start()

    barrier = pltpu.get_barrier_semaphore()

    def greet_seq(j, carry):
        pl.semaphore_signal(barrier, inc=1, device_id=((seq + j) % n_seq, voc), device_id_type=MESH)
        return carry

    def greet_voc(j, carry):
        pl.semaphore_signal(barrier, inc=1, device_id=(seq, (voc + j) % n_voc), device_id_type=MESH)
        return carry

    lax.fori_loop(1, n_seq, greet_seq, 0)
    lax.fori_loop(1, n_voc, greet_voc, 0)
    fgain[0] = fg_p[...].reshape(1, width)
    fgain[1] = fg_r[...].reshape(1, width)
    igain[0] = ing_p[...].reshape(1, width)
    igain[1] = ing_r[...].reshape(1, width)
    stat[...] = jnp.zeros_like(stat)
    prompt_rows = pbuf.shape[2]
    per_prompt = pk_p.shape[1]
    for m, (keys, values) in enumerate(((pk_p, pv_p), (pk_r, pv_r))):
        pbuf[seq, m, :, 0:HD] = keys[...].astype(F32).reshape(prompt_rows, HD).astype(BF16)
        pbuf[seq, m, :, HD : 2 * HD] = values[...].astype(F32).reshape(prompt_rows, HD).astype(BF16)

    starts = [jnp.int32(0)]
    for r in range(rolls):
        starts.append(starts[-1] + lens[r])

    def packed_of(slot):
        packed = slot + (source[0] * BLOCK)
        for b in range(1, rows // BLOCK):
            packed = jnp.where(slot >= b * BLOCK, slot + (source[b] - b) * BLOCK, packed)
        return packed

    def lookup(packed, values):
        found = jnp.full_like(packed, 0) + values[0]
        for r in range(1, rolls):
            found = jnp.where(packed >= starts[r], values[r], found)
        return found

    row_code = packed_of(lax.broadcasted_iota(jnp.int32, (8, rows), 1))
    codes[seq] = row_code
    pl.semaphore_wait(barrier, n_seq - 1 + n_voc - 1)

    def prompt_copy(j):
        peer = (seq + j) % n_seq
        return remote(pbuf.at[seq], pbuf.at[seq], p_s.at[j], p_r.at[seq], peer, voc)

    def code_copy(j):
        peer = (seq + j) % n_seq
        return remote(codes.at[seq], codes.at[seq], c_s.at[j], c_r.at[seq], peer, voc)

    def send_small(j, carry):
        prompt_copy(j).start()
        code_copy(j).start()
        return carry

    lax.fori_loop(1, n_seq, send_small, 0)

    packed_col = packed_of(lax.broadcasted_iota(jnp.int32, (rows, 128), 0))
    first_col = lookup(packed_col, starts)
    prompt_col = lookup(packed_col, [prompt_of[r] for r in range(rolls)])
    target_col = jnp.transpose(
        jnp.broadcast_to(tgt_ref[...].reshape(1, rows).astype(F32), (128, rows))
    ).astype(jnp.int32)
    lane_col = lax.broadcasted_iota(jnp.int32, (rows, 128), 1)
    col = jnp.where(lane_col == 0, first_col, packed_col)
    col = jnp.where(lane_col == 2, prompt_col, col)
    col_ref[...] = jnp.where(lane_col == 3, target_col, col)
    place = packed_col - first_col + per_prompt * n_seq
    angles = place.astype(F32) * freq_ref[...]
    cos_ref[...] = jnp.cos(angles)
    sine = jnp.sin(angles)
    sin_ref[...] = jnp.where(lane_col < HD // 2, -sine, sine)

    def kv_copy(m, src, dst_seq, slot):
        return remote(kv.at[m, src], kv.at[m, src], kv_s.at[m, slot], kv_r.at[m, src], dst_seq, voc)

    def turn(values, gain):
        values = values * lax.rsqrt(jnp.mean(values * values, axis=-1, keepdims=True) + EPSILON) * gain
        return (values * cos_ref[...] + pltpu.roll(values, HD // 2, axis=1) * sin_ref[...]).astype(BF16)

    for m in range(2):
        qg, kg = ((qg_p, kg_p), (qg_r, kg_r))[m]
        loads[4 * m].wait()

        def norm_rows(i, carry, m=m):
            here = pl.ds(pl.multiple_of(i * 32, 32), 32)
            values = hid[m, here, :].astype(F32)
            inv = lax.rsqrt(jnp.mean(values * values, axis=-1, keepdims=True) + EPSILON)
            fin[0, here, :] = (values * inv * igain[m]).astype(BF16)
            return carry

        lax.fori_loop(0, rows // 32, norm_rows, 0)
        for copy in loads[4 * (m + 1) : 4 * (m + 2)]:
            copy.start()
        loads[4 * m + 1].wait()
        loads[4 * m + 2].wait()
        key_rows = turn(dot(fin[0], wk[m]), kg[...])
        kv[m, seq, :, 0:HD] = key_rows
        kv[m, seq, :, HD : 2 * HD] = dot(fin[0], wv[m]).astype(BF16)
        kv_copy(m, seq, sibling, 0).start()

        def send_kv(j, carry, m=m):
            kv_copy(m, seq, ((chip + j) % n_chips) * 2 + core, j).start()
            return carry

        lax.fori_loop(1, n_chips, send_kv, 0)
        loads[4 * m + 3].wait()
        for h in range(0, heads, 2):
            both = dot(fin[0], wq[m, :, h * HD : (h + 2) * HD])
            query[m, h] = turn(both[:, :HD], qg[...])
            query[m, h + 1] = turn(both[:, HD:], qg[...])

    def wait_small(j, carry):
        src = (seq + n_seq - j) % n_seq
        remote(pbuf.at[src], pbuf.at[src], p_s.at[j], p_r.at[src], src, voc).wait_recv()
        remote(codes.at[src], codes.at[src], c_s.at[j], c_r.at[src], src, voc).wait_recv()
        prompt_copy(j).wait_send()
        code_copy(j).wait_send()
        return carry

    lax.fori_loop(1, n_seq, wait_small, 0)
    loads[8].wait()
    loads[9].wait()

    first = col_ref[:, 0:1]
    index = col_ref[:, 1:2]
    prompt = col_ref[:, 2:3]
    prompt_all = n_seq * prompt_rows
    tiles = prompt_all // rows
    per_tile = rows // prompt_rows

    def see(t, carry):
        code = codes[t][0:1, :]
        bias[t] = jnp.where((code >= first) & (code <= index), 0.0, NEGATIVE_FILL)
        return carry

    lax.fori_loop(0, n_seq, see, 0)
    owner = (lax.broadcasted_iota(jnp.int32, (1, rows), 1) % prompt_rows) // per_prompt
    bias[n_seq] = jnp.where(owner == prompt, 0.0, NEGATIVE_FILL)

    def forward_kv(m):
        def chip_step(j, inner):
            src = ((chip + n_chips - j) % n_chips) * 2 + core
            kv_copy(m, src, sibling, 0).wait_recv()
            kv_copy(m, src, sibling, n_chips + j).start()
            return inner

        lax.fori_loop(1, n_chips, chip_step, 0)

    def gathered_kv(m):
        def chip_step(j, inner):
            kv_copy(m, ((chip + n_chips - j) % n_chips) * 2 + (1 - core), sibling, 0).wait_recv()
            return inner

        lax.fori_loop(0, n_chips, chip_step, 0)

    is_end = (voc == 0) | (voc == n_voc - 1)
    middle = 1 + voc // 2
    end = (voc // 2) * 3
    other = 3 - voc

    def rows_of(k, off, count):
        return pl.ds(pl.multiple_of((k % chunks) * CHUNK + off, half), count)

    def partial_sums(m, out):
        values = attended[m]
        for c in range(0, width, 512):
            out[m, :, c : c + 512] = dot(values, wo[m, :, c : c + 512]).astype(BF16)

    def in_copy(k):
        m, here = k // chunks, rows_of(k, 0, CHUNK)
        return remote(inbuf.at[m, here, :], inbuf.at[m, here, :], in_s.at[k], in_r.at[k], seq, middle)

    def prompt_tile(m, t):
        here = pl.ds(t * per_tile, per_tile)
        return pbuf[here, m].reshape(rows, 2 * HD)

    def head_step(m, h):
        rate = HD ** (-0.5)
        q = query[m, h]

        def seen(t, high):
            scores = dot_t(q, kv[m, t, :, 0:HD]) + bias[t]
            kept[t] = scores
            return jnp.maximum(high, jnp.maximum(scores[:, :HD], scores[:, HD:]))

        def seen_prompt(t, high):
            scores = dot_t(q, prompt_tile(m, t)[:, 0:HD]) + bias[n_seq]
            kept[n_seq + t] = scores
            return jnp.maximum(high, jnp.maximum(scores[:, :HD], scores[:, HD:]))

        high = jnp.full((rows, HD), NEGATIVE_FILL, F32)
        high = lax.fori_loop(0, tiles, seen_prompt, high)
        high = lax.fori_loop(0, n_seq, seen, high, unroll=2)
        top = jnp.max(high, axis=-1, keepdims=True)

        def weigh(t, values, state):
            mass, total_value = state
            weights = jnp.exp((kept[t] - top) * rate)
            mass = mass + (weights[:, :HD] + weights[:, HD:])
            return (mass, total_value + dot(weights.astype(BF16), values))

        state = (jnp.zeros((rows, HD), F32), jnp.zeros((rows, HD), F32))
        state = lax.fori_loop(
            0, tiles, lambda t, c: weigh(n_seq + t, prompt_tile(m, t)[:, HD:], c), state
        )
        mass, value = lax.fori_loop(
            0, n_seq, lambda t, c: weigh(t, kv[m, t, :, HD : 2 * HD], c), state, unroll=2
        )
        attended[m, :, h * HD : (h + 1) * HD] = (value / jnp.sum(mass, axis=-1, keepdims=True)).astype(BF16)

    forward_kv(0)
    gathered_kv(0)
    for m in range(2):
        if m == 1:
            gathered_kv(1)
        for h in range(heads):
            head_step(m, h)
            if m == 0 and h == heads // 2:
                forward_kv(1)

        @pl.when(is_end)
        def _(m=m):
            partial_sums(m, inbuf)
            if m == 0:
                in_copy(0).start()
                in_copy(1).start()

        @pl.when(jnp.logical_not(is_end))
        def _(m=m):
            partial_sums(m, own)

    loads[10].wait()
    loads[11].wait()

    lanes = lax.broadcasted_iota(jnp.int32, (2 * CHUNK, 128), 1)

    def head_pair(k):
        m, here = k // chunks, rows_of(k, 0, 2 * CHUNK)
        logits = dot(fin[m, here, :], hd[m])
        top = jnp.max(logits, axis=-1, keepdims=True)
        mass = jnp.sum(jnp.exp(logits - top), axis=-1, keepdims=True)
        word = voc * words + lax.broadcasted_iota(jnp.int32, (2 * CHUNK, words), 1)
        target = col_ref[here, 3:4]
        hit = jnp.sum(jnp.where(word == target, logits, 0.0), axis=-1, keepdims=True)
        old = stat[here, :]
        old = jnp.where(lanes == 3 * m, top, old)
        old = jnp.where(lanes == 3 * m + 1, mass, old)
        stat[here, :] = jnp.where(lanes == 3 * m + 2, hit, old)

    mine = (voc - 1) * half
    theirs = half - mine

    def x_copy(k):
        return remote(inbuf.at[k // chunks, rows_of(k, theirs, half), :], xr.at[k], x_s.at[k], x_r.at[k], seq, other)

    def f_copy(k, off):
        ref = fin.at[k // chunks, rows_of(k, off, half), :]
        return remote(ref, ref, f_s.at[k], f_r.at[k], seq, other)

    def e_copy(k, off, which):
        ref = fin.at[k // chunks, rows_of(k, off, half), :]
        return remote(ref, ref, e_s.at[2 * k + which], e_r.at[2 * k + which], seq, end)

    @pl.when(is_end)
    def _():
        def issue(k, carry):
            in_copy(k - 2).wait_send()
            in_copy(k).start()
            return carry

        lax.fori_loop(2, total, issue, 0)
        first_off = (middle - 1) * half

        def landed(k):
            for which, off in ((0, first_off), (1, half - first_off)):
                ref = fin.at[k // chunks, rows_of(k, off, half), :]
                remote(ref, ref, e_s.at[2 * k + which], e_r.at[2 * k + which], seq, middle).wait_recv()

        def step(i, carry):
            landed(2 * i)
            landed(2 * i + 1)
            head_pair(2 * i)
            return carry

        lax.fori_loop(0, total // 2, step, 0)
        in_copy(total - 2).wait_send()
        in_copy(total - 1).wait_send()

    @pl.when(jnp.logical_not(is_end))
    def _():
        def pass_on(k):
            f_copy(k, theirs).wait_recv()
            e_copy(k, theirs, 1).start()

            @pl.when(k % 2 == 1)
            def _():
                head_pair(k - 1)

        def step(k, carry):
            m = k // chunks
            pltpu.make_async_remote_copy(
                src_ref=inbuf.at[m, rows_of(k, 0, CHUNK), :],
                dst_ref=inbuf.at[m, rows_of(k, 0, CHUNK), :],
                send_sem=in_s.at[k],
                recv_sem=in_r.at[k],
                device_id=(seq, end),
                device_id_type=MESH,
            ).wait_recv()
            away = rows_of(k, theirs, half)
            inbuf[m, away, :] = (own[m, away, :].astype(F32) + inbuf[m, away, :].astype(F32)).astype(BF16)
            x_copy(k).start()

            @pl.when(k > 0)
            def _():
                complete(k - 1)

            @pl.when(k > 1)
            def _():
                pass_on(k - 2)

            return carry

        def complete(k):
            m, here = k // chunks, rows_of(k, mine, half)
            x_copy(k).wait_recv()
            mixed = own[m, here, :].astype(F32) + inbuf[m, here, :].astype(F32)
            values = hid[m, here, :].astype(F32) + (mixed + xr[k].astype(F32))
            inv = lax.rsqrt(jnp.mean(values * values, axis=-1, keepdims=True) + EPSILON)
            fin[m, here, :] = (values * inv * fgain[m]).astype(BF16)
            f_copy(k, mine).start()
            e_copy(k, mine, 0).start()

        lax.fori_loop(0, total, step, 0)
        complete(total - 1)
        pass_on(jnp.int32(total - 2))
        pass_on(jnp.int32(total - 1))

        def drain(k, carry):
            x_copy(k).wait_send()
            f_copy(k, mine).wait_send()
            e_copy(k, mine, 0).wait_send()
            e_copy(k, theirs, 1).wait_send()
            return carry

        lax.fori_loop(0, total, drain, 0)

    sbuf[voc] = jnp.transpose(stat[...])[0:8, :]

    def stat_copy(j):
        return remote(sbuf.at[voc], sbuf.at[voc], st_s.at[j], st_r.at[voc], seq, (voc + j) % n_voc)

    for j in range(1, n_voc):
        stat_copy(j).start()
    for m in range(2):
        def drain_kv(j, carry, m=m):
            kv_copy(m, seq, sibling, j).wait_send()
            return carry

        lax.fori_loop(0, n_chips, drain_kv, 0)
        lax.fori_loop(n_chips + 1, 2 * n_chips, drain_kv, 0)
    for j in range(1, n_voc):
        src = (voc + n_voc - j) % n_voc
        remote(sbuf.at[src], sbuf.at[src], st_s.at[j], st_r.at[src], seq, src).wait_recv()
    parts = [sbuf[v] for v in range(n_voc)]

    def score(m):
        top = functools.reduce(jnp.maximum, [p[3 * m : 3 * m + 1] for p in parts])
        mass = sum(p[3 * m + 1 : 3 * m + 2] * jnp.exp(p[3 * m : 3 * m + 1] - top) for p in parts)
        hit = sum(p[3 * m + 2 : 3 * m + 3] for p in parts)
        return hit - (top + jnp.log(mass))

    diff = score(0) - score(1)
    diff_ref[...] = diff.reshape(rows)
    packed_row = packed_of(lax.broadcasted_iota(jnp.int32, (1, rows), 1))
    per_token = diff / lookup(packed_row, [lens[r] for r in range(rolls)]).astype(F32)
    slot = lookup(packed_row, [jnp.int32(r) for r in range(rolls)])
    lane = lax.broadcasted_iota(jnp.int32, (8, 128), 1)
    block = jnp.zeros((8, 128), F32)
    for r in range(rolls):
        piece = jnp.sum(jnp.where(slot == r, per_token, 0.0), axis=1, keepdims=True)
        block = jnp.where(lane == slot_of[r], piece, block)
    rbuf[seq] = block

    def roll_copy(j):
        return remote(rbuf.at[seq], rbuf.at[seq], ro_s.at[j], ro_r.at[seq], (seq + j) % n_seq, voc)

    def start_roll(j, carry):
        roll_copy(j).start()
        return carry

    def wait_roll(j, carry):
        src = (seq + n_seq - j) % n_seq
        remote(rbuf.at[src], rbuf.at[src], ro_s.at[j], ro_r.at[src], src, voc).wait_recv()
        return carry

    def drain_roll(j, carry):
        roll_copy(j).wait_send()
        return carry

    lax.fori_loop(1, n_seq, start_roll, 0)
    lax.fori_loop(1, n_seq, wait_roll, 0)
    means = jnp.sum(rbuf[...], axis=0)
    for r in range(rolls):
        mean_ref[r] = means[0, r]
    lax.fori_loop(1, n_seq, drain_roll, 0)
    for j in range(1, n_voc):
        stat_copy(j).wait_send()


def local(
    policy_hidden,
    reference_hidden,
    targets,
    lengths,
    block_source,
    rollout_prompt,
    rollout_slot,
    policy_input_gain,
    policy_query_weight,
    policy_key_weight,
    policy_value_weight,
    policy_query_gain,
    policy_key_gain,
    policy_out_weight,
    policy_final_gain,
    policy_head,
    policy_prompt_keys,
    policy_prompt_values,
    reference_input_gain,
    reference_query_weight,
    reference_key_weight,
    reference_value_weight,
    reference_query_gain,
    reference_key_gain,
    reference_out_weight,
    reference_final_gain,
    reference_head,
    reference_prompt_keys,
    reference_prompt_values,
):
    n_seq = lax.axis_size("seq")
    rows, width = policy_hidden.shape
    rolls = lengths.shape[0]
    heads = policy_query_weight.shape[1] // HD
    words = policy_head.shape[1]
    chunks = rows // CHUNK
    total = 2 * chunks
    prompt_count, prefix_local = policy_prompt_keys.shape[:2]
    prompt_rows = prompt_count * prefix_local

    frequency = ROPE_BASE ** (-2.0 * np.arange(HD // 2, dtype=np.float32) / HD)
    frequency = np.concatenate([frequency, frequency]).astype(np.float32)[None]
    smem = pl.BlockSpec(memory_space=pltpu.SMEM)
    vmem = pl.BlockSpec(memory_space=pltpu.VMEM)
    hbm = pl.BlockSpec(memory_space=pl.ANY)
    dma = pltpu.SemaphoreType.DMA
    n_chips = n_seq // 2
    return pl.pallas_call(
        functools.partial(kernel, n_seq, rolls),
        out_shape=(
            jax.ShapeDtypeStruct((rows,), F32),
            jax.ShapeDtypeStruct((rolls,), F32),
        ),
        in_specs=[smem] * 4 + [vmem] * 6 + [hbm] * 2 + [vmem] * 8 + [hbm] * 10,
        out_specs=(vmem, smem),
        scratch_shapes=[
            pltpu.VMEM((2, width, heads * HD), BF16),
            pltpu.VMEM((2, width, HD), BF16),
            pltpu.VMEM((2, width, HD), BF16),
            pltpu.VMEM((2, heads * HD, width), BF16),
            pltpu.VMEM((2, width, words), BF16),
            pltpu.VMEM((2, rows, width), BF16),
            pltpu.VMEM((2, 1, width), F32),
            pltpu.VMEM((2, heads, rows, HD), BF16),
            pltpu.VMEM((2, n_seq, rows, 2 * HD), BF16),
            pltpu.VMEM((n_seq, 2, prompt_rows, 2 * HD), BF16),
            pltpu.VMEM((n_seq, 8, rows), jnp.int32),
            pltpu.VMEM((n_seq + 1, rows, rows), F32),
            pltpu.VMEM((n_seq + n_seq * prompt_rows // rows, rows, rows), F32),
            pltpu.VMEM((rows, 128), jnp.int32),
            pltpu.VMEM((rows, 128), F32),
            pltpu.VMEM((rows, 128), F32),
            pltpu.VMEM((2, 1, width), F32),
            pltpu.VMEM((2, rows, heads * HD), BF16),
            pltpu.VMEM((2, rows, width), BF16),
            pltpu.VMEM((total, CHUNK // 2, width), BF16),
            pltpu.VMEM((2, rows, width), BF16),
            pltpu.VMEM((2, rows, width), BF16),
            pltpu.VMEM((rows, 128), F32),
            pltpu.VMEM((4, 8, rows), F32),
            pltpu.VMEM((n_seq, 8, 128), F32),
            dma((12,)),
            dma((2, n_seq)),
            dma((2, n_seq)),
            dma((n_seq,)),
            dma((n_seq,)),
            dma((n_seq,)),
            dma((n_seq,)),
            dma((total,)),
            dma((total,)),
            dma((total,)),
            dma((total,)),
            dma((total,)),
            dma((total,)),
            dma((2 * total,)),
            dma((2 * total,)),
            dma((4,)),
            dma((4,)),
            dma((n_seq,)),
            dma((n_seq,)),
        ],
        compiler_params=pltpu.CompilerParams(
            collective_id=0, has_side_effects=True, vmem_limit_bytes=60 * 1024 * 1024
        ),
    )(
        lengths,
        block_source,
        rollout_prompt,
        rollout_slot,
        targets,
        frequency,
        policy_prompt_keys,
        policy_prompt_values,
        reference_prompt_keys,
        reference_prompt_values,
        policy_hidden,
        reference_hidden,
        policy_input_gain,
        reference_input_gain,
        policy_query_gain[None],
        reference_query_gain[None],
        policy_key_gain[None],
        reference_key_gain[None],
        policy_final_gain,
        reference_final_gain,
        policy_query_weight,
        reference_query_weight,
        policy_key_weight,
        reference_key_weight,
        policy_value_weight,
        reference_value_weight,
        policy_out_weight,
        reference_out_weight,
        policy_head,
        reference_head,
    )


def solution(mesh):
    model_specs = (
        P(),
        P(None, "vocab"),
        P(None, "vocab"),
        P(None, "vocab"),
        P(),
        P(),
        P("vocab", None),
        P(),
        P(None, "vocab"),
        P(None, "seq", "vocab"),
        P(None, "seq", "vocab"),
    )
    return jax.shard_map(
        local,
        mesh=mesh,
        in_specs=(P("seq", None), P("seq", None), P("seq"), P(), P("seq"), P(), P()) + model_specs * 2,
        out_specs=(P("seq"), P()),
        check_vma=False,
    )
```
